256 devices in a mesh: pages: 128 (over y_lo, x, z, core), tok: 2 (over y_hi).
Axes of the slice: x: 4, y: 4 (y_hi: 2, y_lo: 2; y = y_hi * 2 + y_lo), z: 8, core: 2. Of those that a mesh axis runs over, the one named last changes fastest.
Arguments:
- queries: bfloat16 [256, 32, 128], P('pages'), may hold values from -50 to 50
- pages: bfloat16 [128, 1024, 128], P('pages', 'tok'), may hold values from -10 to 10
- pad_counts: int32 [128], P('pages'), may hold values from 0 to 511
- labels: int32 [256, 128], P(None, 'pages'), may hold values 0 or 1
Outputs:
- query_grad: float32 [256, 32, 128], P('pages')
- page_grad: float32 [128, 1024, 128], P('pages', 'tok')
- page_loss: float32 [128], P('pages')
The draws below stay inside these ranges and needn't reach their ends.
All inputs are finite; a program needn't handle non-finite values. No bound on the sum of `labels` on one device may be relied on, other than what follows from the above.
Results may differ from the reference program's by a relative error of at most 0.0025.
Values may be sent and summed in bfloat16 or wider, within the bound.
A program may use at most 64 MiB of HBM per device.

```python
import math
import jax
import jax.numpy as jnp
from jax import lax

E = 128
LQ = 32
LP = 1024
NQ = 256
NP = 128


def shared_tables(key):
    page_key = jax.random.fold_in(key, 7101)
    query_key = jax.random.fold_in(key, 7102)
    pages = jnp.clip(jax.random.normal(page_key, (NP, LP, E), jnp.float32), -6.0, 6.0)
    queries = jnp.clip(jax.random.normal(query_key, (NQ, LQ, E), jnp.float32), -6.0, 6.0)
    return (pages, queries)


def draw_queries(key, part):
    return shared_tables(key)[1].astype(jnp.bfloat16)


def draw_pages(key, part):
    return shared_tables(key)[0].astype(jnp.bfloat16)


def touch_ends(entries, stream_key, smallest, largest):
    place = [jax.random.randint(jax.random.fold_in(stream_key, axis), (), 0, length) for axis, length in enumerate(entries.shape)]
    main_axis = entries.shape.index(max(entries.shape))
    beside = place[:main_axis] + [(place[main_axis] + 1) % entries.shape[main_axis]] + place[main_axis + 1:]
    return entries.at[tuple(place)].set(smallest).at[tuple(beside)].set(largest)


def setup_inputs(seed: int = 0) -> dict:
    key_of = jax.random.split(jax.random.key(seed), 5)
    queries = draw_queries(jax.random.fold_in(key_of[4], 71), 0)
    pages = draw_pages(jax.random.fold_in(key_of[4], 71), 0)
    pad_counts = touch_ends(jax.random.randint(key_of[2], (NP,), 0, LP // 2), jax.random.fold_in(key_of[2], 1), 0, (LP // 2) - 1).astype(jnp.int32)
    labels = touch_ends((jax.random.randint(key_of[3], (NQ, NP), 0, 16) < 1).astype(jnp.int32), jax.random.fold_in(key_of[3], 1), 0, 1)
    return dict(queries=queries, pages=pages, pad_counts=pad_counts, labels=labels)


MASKED = -1.0e9
LOGIT_SPAN = 8.0
CENTRE_SHIFT = 0.5
FILL_SHARE = 0.75


def page_scores(query_rows, page_rows, usable):
    raw = jnp.dot(query_rows, page_rows.T, preferred_element_type=jnp.float32) * (E ** -0.5)
    return jnp.where(usable[None, :], raw, MASKED)


def smooth_max(scores):
    highest = jnp.max(scores, axis=1)
    return highest + jnp.log(jnp.sum(jnp.exp(scores - highest[:, None]), axis=1))


def reference(queries, pages, pad_counts, labels):
    query_rows = queries.reshape(NQ * LQ, E)
    positions = jnp.arange(LP, dtype=jnp.int32)
    usable = positions[None, :] < (LP - pad_counts)[:, None]

    def forward_page(packed):
        page_rows, page_usable = packed
        return smooth_max(page_scores(query_rows, page_rows, page_usable))

    smooth = lax.map(forward_page, (pages, usable))
    similarity = smooth.reshape(NP, NQ, LQ).sum(axis=2).T
    label_sign = 2.0 * labels.astype(jnp.float32) - 1.0
    logit_gain = LOGIT_SPAN / LQ
    centre = LQ * (CENTRE_SHIFT + math.log(FILL_SHARE * LP))
    logits = logit_gain * (similarity - centre)
    page_loss = jnp.sum(jax.nn.softplus(-label_sign * logits), axis=0)
    slope = logit_gain * (-label_sign * jax.nn.sigmoid(-label_sign * logits))
    row_slope = jnp.repeat(slope.T, LQ, axis=1)

    def backward_page(running, packed):
        page_rows, page_usable, page_smooth, page_slope = packed
        scores = page_scores(query_rows, page_rows, page_usable)
        weights = jnp.where(page_usable[None, :], jnp.exp(scores - page_smooth[:, None]), 0.0)
        scaled = (weights * page_slope[:, None]).astype(jnp.bfloat16)
        running = running + jnp.dot(scaled, page_rows, preferred_element_type=jnp.float32) * (E ** -0.5)
        page_term = jnp.dot(scaled.T, query_rows, preferred_element_type=jnp.float32) * (E ** -0.5)
        return running, page_term

    query_sum, page_grad = lax.scan(backward_page, jnp.zeros((NQ * LQ, E), jnp.float32), (pages, usable, smooth, row_slope))
    return query_sum.reshape(NQ, LQ, E), page_grad, page_loss
```

```python
import functools
import math

import jax
import jax.numpy as jnp
from jax import lax
from jax.experimental import pallas as pl
from jax.experimental.pallas import tpu as pltpu
from jax.sharding import Mesh
from jax.sharding import PartitionSpec as P

MESH = pl.DeviceIdType.MESH
PAGES = ("yl", "x", "z", "core")

MASKED = -1.0e9
LOGIT_SPAN = 8.0
CENTRE_SHIFT = 0.5
FILL_SHARE = 0.75

NX, NZ = 4, 8
E, LQ, LP = 128, 32, 1024
HALF = LP // 2
ROWS = NZ * LQ
TILE = 256
F32, BF16 = jnp.float32, jnp.bfloat16

AUX, SIB_PAGE, FAR_PAGE, SIB_FAR_PAGE, TILE_Y = range(5)
TILE_Z = 5
TILE_Z_OTHER = TILE_Z + NZ
OWN_R, OWN_L, OTHER_R, OTHER_L, FWD_R, FWD_L = range(TILE_Z_OTHER + NZ, TILE_Z_OTHER + NZ + 6)
SUM_A, SUM_B, SUM_AR, SUM_BL, SUM_BR, SUM_AL, SUM_Y = range(FWD_L + 1, FWD_L + 8)
SUM_Z = SUM_Y + 1
FINAL_Q = SUM_Z + NZ
PG_FAR, PG_NEAR, LOSS_SIB, PG_Y, LOSS_Y = range(FINAL_Q + 1, FINAL_Q + 6)
COPIES = LOSS_Y + 1


def rows_of(pieces, shape):
    row = lax.broadcasted_iota(jnp.int32, shape, 0)
    total = jnp.zeros(shape, F32)
    for index, piece in enumerate(pieces):
        total = jnp.where(row == index, piece, total)
    return total


def dot(left, right, dims):
    return lax.dot_general(left, right, (dims, ((), ())), preferred_element_type=F32)


def kernel(
    q_ref, page_ref, pad_ref, label_ref,
    qg_ref, pg_ref, loss_ref,
    q_all, p_all, p_turned, bias, aux, aux_sib, labels_wide, group_ones,
    raw, weights, pg_sum, loss_sum,
    qg, in_a, in_b, in_left, in_right, in_y, turned, in_z, fin, in_fin,
    pg_sib, pg_out, pg_far, loss_out, loss_sib, loss_far,
    send_sem, recv_sem,
):
    yl, x, z = lax.axis_index("yl"), lax.axis_index("x"), lax.axis_index("z")
    core, yh = lax.axis_index("core"), lax.axis_index("yh")
    oyl, ocore, oyh = 1 - yl, 1 - core, 1 - yh
    right, left, across = lax.rem(x + 1, NX), lax.rem(x + 3, NX), lax.rem(x + 2, NX)

    def zplus(step):
        return lax.rem(z + step, NZ)

    def copy(source, target, index, where):
        return pltpu.make_async_remote_copy(
            src_ref=source,
            dst_ref=target,
            send_sem=send_sem.at[index],
            recv_sem=recv_sem.at[index],
            device_id=where,
            device_id_type=MESH,
        )

    to_sib, to_far, to_y = {"core": ocore}, {"yh": oyh}, {"yl": oyl}
    to_right, to_left = {"x": right}, {"x": left}

    barrier = pltpu.get_barrier_semaphore()
    partners = [to_sib, to_far, to_y, to_right, to_left]
    partners += [{"z": zplus(step)} for step in range(1, NZ)]
    for where in partners:
        pl.semaphore_signal(barrier, inc=1, device_id=where, device_id_type=MESH)

    own, other = yl * NX + x, oyl * NX + x
    q_all[own, z] = q_ref[yh]
    p_all[core, yh] = page_ref[0]
    row = lax.broadcasted_iota(jnp.int32, (8, 2 * E), 0)
    aux[...] = jnp.where(row == 0, label_ref[...].astype(F32), pad_ref[0].astype(F32))
    pl.semaphore_wait(barrier, len(partners))

    c_tile_y = copy(q_all.at[own, z], q_all.at[own, z], TILE_Y, to_y)
    c_tile_z = [
        copy(q_all.at[own, z], q_all.at[own, z], TILE_Z + step, {"z": zplus(step)})
        for step in range(1, NZ)
    ]
    c_tile_zo = [
        copy(q_all.at[other, z], q_all.at[other, z], TILE_Z_OTHER + step, {"z": zplus(step)})
        for step in range(1, NZ)
    ]
    c_far_page = copy(p_all.at[core, yh], p_all.at[core, yh], FAR_PAGE, to_far)
    c_sib_page = copy(p_all.at[core, yh], p_all.at[core, yh], SIB_PAGE, to_sib)
    c_sib_far = copy(p_all.at[core, oyh], p_all.at[core, oyh], SIB_FAR_PAGE, to_sib)
    c_aux = copy(aux, aux_sib, AUX, to_sib)
    c_own_r = copy(q_all.at[own], q_all.at[own], OWN_R, to_right)
    c_own_l = copy(q_all.at[own], q_all.at[own], OWN_L, to_left)
    c_other_r = copy(q_all.at[other], q_all.at[other], OTHER_R, to_right)
    c_other_l = copy(q_all.at[other], q_all.at[other], OTHER_L, to_left)
    from_left, from_right = yl * NX + left, oyl * NX + right
    c_fwd_r = copy(q_all.at[from_left], q_all.at[from_left], FWD_R, to_right)
    c_fwd_l = copy(q_all.at[from_right], q_all.at[from_right], FWD_L, to_left)

    c_tile_y.start()
    for each in c_tile_z:
        each.start()
    c_far_page.start()
    c_sib_page.start()
    c_aux.start()
    c_tile_y.wait_recv()
    for each in c_tile_zo:
        each.start()

    lane = lax.broadcasted_iota(jnp.int32, (2 * E, ROWS), 1)
    line = lax.broadcasted_iota(jnp.int32, (2 * E, ROWS), 0)
    group_ones[...] = (line // LQ == lane // LQ).astype(F32).astype(BF16)
    c_aux.wait_recv()
    position = lax.broadcasted_iota(jnp.int32, (LP, E), 0)
    wanted = (line % LQ == (lane // LQ) * 4 + 2 * core + yh).astype(F32).astype(BF16)
    block_row = lax.broadcasted_iota(jnp.int32, (8, 2 * E), 0)
    block_of = lax.broadcasted_iota(jnp.int32, (8, 2 * E), 1) // LQ
    for place, holder in ((core, aux), (ocore, aux_sib)):
        pad = holder[1:2, 0:E].astype(jnp.int32)
        bias[place] = jnp.where(position < LP - pad, 0.0, MASKED)
        spread = jnp.where(block_row == block_of, holder[0:1, :], 0.0).astype(BF16)
        labels_wide[place] = dot(spread, wanted, ((1,), (0,)))
    pg_sum[...] = jnp.zeros_like(pg_sum)
    loss_sum[...] = jnp.zeros_like(loss_sum)

    for each in c_tile_z:
        each.wait_recv()
    c_own_r.start()
    c_own_l.start()
    for each in c_tile_zo:
        each.wait_recv()
    c_other_r.start()
    c_other_l.start()
    c_far_page.wait_recv()
    c_sib_far.start()
    c_own_r.wait_recv()
    c_fwd_r.start()
    c_other_l.wait_recv()
    c_fwd_l.start()
    c_sib_page.wait_recv()
    c_sib_far.wait_recv()
    for place in range(2):
        for half in range(2):
            turned_half = p_all[place, half].astype(F32).T
            p_turned[place, :, half * HALF : (half + 1) * HALF] = turned_half.astype(BF16)
    c_own_l.wait_recv()
    c_other_r.wait_recv()
    c_fwd_r.wait_recv()
    c_fwd_l.wait_recv()

    score_scale = E ** (-0.5)
    power = score_scale * math.log2(math.e)
    gain = LOGIT_SPAN / LQ
    centre = LQ * (CENTRE_SHIFT + math.log(FILL_SHARE * LP))

    c_sum_a = copy(qg.at[0], in_a, SUM_A, to_right)
    c_sum_b = copy(qg.at[1], in_b, SUM_B, to_left)
    c_sum_ar = copy(qg.at[2], in_left.at[0], SUM_AR, to_right)
    c_sum_bl = copy(qg.at[3], in_right.at[1], SUM_BL, to_left)
    c_sum_br = copy(qg.at[4], in_left.at[1], SUM_BR, to_right)
    c_sum_al = copy(qg.at[5], in_right.at[0], SUM_AL, to_left)
    c_sum_y = copy(qg.at[6], in_y, SUM_Y, to_y)

    def block(step, carry):
        owner_x = jnp.where(
            step < 2,
            across,
            jnp.where(step >= 6, x, jnp.where((step == 2) | (step == 4), right, left)),
        )
        owner_y = jnp.where((step == 0) | (step == 2) | (step == 5) | (step == 7), yl, oyl)
        chunk = owner_y * NX + owner_x
        rows = q_all[chunk].reshape(ROWS, E)

        tops = []
        for place in range(2):
            top = jnp.full((8, ROWS), -3.0e38, F32)
            for tile in range(LP // TILE):
                span = pl.ds(tile % (HALF // TILE) * TILE, TILE)
                scores = dot(p_all[place, tile * TILE // HALF, span], rows, ((1,), (1,)))
                hidden = bias[place, tile * TILE : (tile + 1) * TILE]
                scores = scores + jnp.concatenate([hidden, hidden], axis=1)
                raw[place, tile * TILE : (tile + 1) * TILE] = scores
                top = jnp.maximum(top, jnp.max(scores.reshape(TILE // 8, 8, ROWS), axis=0))
            tops.append(jnp.max(top, axis=0, keepdims=True))
        sums = []
        for place in range(2):
            total = jnp.zeros((8, ROWS), F32)
            for tile in range(LP // TILE):
                span = slice(tile * TILE, (tile + 1) * TILE)
                weight = jnp.exp2((raw[place, span] - tops[place]) * power)
                weights[place, span] = weight.astype(BF16)
                total = total + jnp.sum(weight.reshape(TILE // 8, 8, ROWS), axis=0)
            sums.append(jnp.sum(total, axis=0, keepdims=True))

        top2, sum2 = rows_of(tops, (8, ROWS)), rows_of(sums + [1.0] * 6, (8, ROWS))
        smooth = top2 * score_scale + jnp.log(sum2)
        high = smooth.astype(BF16)
        rest = smooth - high.astype(F32)
        middle = rest.astype(BF16)
        low = (rest - middle.astype(F32)).astype(BF16)
        ones = group_ones[...]
        similarity = (
            dot(low, ones, ((1,), (0,))) + dot(middle, ones, ((1,), (0,)))
        ) + dot(high, ones, ((1,), (0,)))
        label_rows = [labels_wide[place, pl.ds(chunk, 1)] for place in range(2)]
        sign = 2.0 * rows_of(label_rows, (8, ROWS)) - 1.0
        lean = -sign * (gain * (similarity - centre))
        small = jnp.exp(-jnp.abs(lean))
        loss_sum[...] += jnp.maximum(lean, 0.0) + jnp.log1p(small)
        slope = -gain * sign * (jnp.where(lean >= 0.0, 1.0, small) / (1.0 + small))
        factor = slope / sum2
        columns = factor.T

        gradient = jnp.zeros((E, ROWS), F32)
        rows32 = rows.astype(F32)
        for place in range(2):
            gradient = gradient + factor[place : place + 1] * dot(
                p_turned[place], weights[place], ((1,), (0,))
            )
            scaled = (rows32 * columns[:, place : place + 1]).astype(BF16)
            pg_sum[place] += dot(weights[place], scaled, ((1,), (0,)))
        qg[step] = gradient

        @pl.when(step == 0)
        def _():
            c_sum_a.start()

        @pl.when(step == 1)
        def _():
            c_sum_b.start()

        @pl.when(step == 2)
        def _():
            c_sum_a.wait_recv()
            qg[2] += in_a[...]
            c_sum_ar.start()

        @pl.when(step == 3)
        def _():
            c_sum_b.wait_recv()
            qg[3] += in_b[...]
            c_sum_bl.start()

        @pl.when(step == 4)
        def _():
            c_sum_br.start()

        @pl.when(step == 5)
        def _():
            c_sum_al.start()

        @pl.when(step == 6)
        def _():
            c_sum_bl.wait_recv()
            c_sum_br.wait_recv()
            qg[6] += in_left[1] + in_right[1]
            c_sum_y.start()

        return carry

    lax.fori_loop(0, 8, block, 0)

    near, far = pl.ds(yh * HALF, HALF), pl.ds(oyh * HALF, HALF)
    c_pg_far = copy(pg_sum.at[ocore, far], pg_sib.at[0], PG_FAR, to_sib)
    c_pg_near = copy(pg_sum.at[ocore, near], pg_sib.at[1], PG_NEAR, to_sib)
    c_loss_sib = copy(loss_out.at[0], loss_sib, LOSS_SIB, to_sib)
    c_pg_y = copy(pg_out, pg_far, PG_Y, to_far)
    c_loss_y = copy(loss_out.at[1], loss_far, LOSS_Y, to_far)
    c_pg_far.start()
    c_pg_near.start()
    mark = lax.broadcasted_iota(jnp.int32, (8, ROWS), 1) % LQ == 0
    losses = jnp.sum(jnp.where(mark, loss_sum[...], 0.0), axis=1, keepdims=True)
    first, second = losses[0:1], losses[1:2]
    own_loss = jnp.where(core == 0, first, second)
    sib_loss = jnp.where(core == 0, second, first)
    loss_out[0] = jnp.broadcast_to(sib_loss, (8, E))
    c_loss_sib.start()

    c_sum_ar.wait_recv()
    c_sum_al.wait_recv()
    c_sum_y.wait_recv()
    total = ((qg[7] + in_left[0]) + (in_right[0] + in_y[...])) * score_scale
    for part in range(2):
        turned[part * 4 : part * 4 + 4] = total[:, part * E : (part + 1) * E].T.reshape(4, LQ, E)
    c_sum_z = [
        copy(turned.at[zplus(step)], in_z.at[step], SUM_Z + step, {"z": zplus(step)})
        for step in range(1, NZ)
    ]
    for each in c_sum_z:
        each.start()

    c_pg_far.wait_recv()
    pg_out[...] = pg_sum[core, far] + pg_sib[0]
    c_pg_y.start()
    c_loss_sib.wait_recv()
    loss_out[1] = jnp.broadcast_to(own_loss, (8, E)) + loss_sib[...]
    c_loss_y.start()

    for each in c_sum_z:
        each.wait_recv()
    mine = turned[z]
    for step in range(1, NZ):
        mine = mine + in_z[step]
    fin[...] = mine
    c_fin = copy(fin, in_fin, FINAL_Q, to_far)
    c_fin.start()
    qg_ref[yh] = mine
    c_pg_near.wait_recv()
    near_sum = pg_sum[core, near] + pg_sib[1]
    c_fin.wait_recv()
    qg_ref[oyh] = in_fin[...]
    c_loss_y.wait_recv()
    loss_ref[0] = jnp.max(loss_out[1, 0:1, 0:1] + loss_far[0:1, 0:1])
    c_pg_y.wait_recv()
    pg_ref[0] = (near_sum + pg_far[...]) * score_scale

    sent = [c_tile_y, c_far_page, c_sib_page, c_sib_far, c_aux, c_own_r, c_own_l, c_other_r]
    sent += [c_other_l, c_fwd_r, c_fwd_l, *c_tile_z, *c_tile_zo]
    sent += [c_sum_a, c_sum_b, c_sum_ar, c_sum_bl, c_sum_br, c_sum_al, c_sum_y, *c_sum_z]
    sent += [c_fin, c_pg_far, c_pg_near, c_loss_sib, c_pg_y, c_loss_y]
    for each in sent:
        each.wait_send()


def on_device(queries, pages, pad_counts, labels):
    vmem = pl.BlockSpec(memory_space=pltpu.VMEM)
    smem = pl.BlockSpec(memory_space=pltpu.SMEM)
    scratch = [
        pltpu.VMEM((8, NZ, LQ, E), BF16),
        pltpu.VMEM((2, 2, HALF, E), BF16),
        pltpu.VMEM((2, E, LP), BF16),
        pltpu.VMEM((2, LP, E), F32),
        pltpu.VMEM((8, 2 * E), F32),
        pltpu.VMEM((8, 2 * E), F32),
        pltpu.VMEM((2, 8, ROWS), F32),
        pltpu.VMEM((2 * E, ROWS), BF16),
        pltpu.VMEM((2, LP, ROWS), F32),
        pltpu.VMEM((2, LP, ROWS), BF16),
        pltpu.VMEM((2, LP, E), F32),
        pltpu.VMEM((8, ROWS), F32),
        pltpu.VMEM((8, E, ROWS), F32),
        pltpu.VMEM((E, ROWS), F32),
        pltpu.VMEM((E, ROWS), F32),
        pltpu.VMEM((2, E, ROWS), F32),
        pltpu.VMEM((2, E, ROWS), F32),
        pltpu.VMEM((E, ROWS), F32),
        pltpu.VMEM((NZ, LQ, E), F32),
        pltpu.VMEM((NZ, LQ, E), F32),
        pltpu.VMEM((LQ, E), F32),
        pltpu.VMEM((LQ, E), F32),
        pltpu.VMEM((2, HALF, E), F32),
        pltpu.VMEM((HALF, E), F32),
        pltpu.VMEM((HALF, E), F32),
        pltpu.VMEM((2, 8, E), F32),
        pltpu.VMEM((8, E), F32),
        pltpu.VMEM((8, E), F32),
        pltpu.SemaphoreType.DMA((COPIES,)),
        pltpu.SemaphoreType.DMA((COPIES,)),
    ]
    flops = 3 * 2 * (8 * ROWS) * (2 * LP) * E
    return pl.pallas_call(
        kernel,
        out_shape=(
            jax.ShapeDtypeStruct(queries.shape, F32),
            jax.ShapeDtypeStruct(pages.shape, F32),
            jax.ShapeDtypeStruct((1,), F32),
        ),
        in_specs=[vmem, vmem, smem, vmem],
        out_specs=(vmem, vmem, smem),
        scratch_shapes=scratch,
        compiler_params=pltpu.CompilerParams(
            collective_id=0, has_side_effects=True, vmem_limit_bytes=48 * 1024 * 1024
        ),
        cost_estimate=pl.CostEstimate(
            flops=flops, bytes_accessed=2 << 20, transcendentals=8 * ROWS * 2 * LP
        ),
    )(queries, pages, pad_counts, labels.reshape(1, -1))


def solution(mesh):
    finer = Mesh(mesh.devices.reshape(2, NX, NZ, 2, 2), (*PAGES, "yh"))
    return jax.shard_map(
        on_device,
        mesh=finer,
        in_specs=(P(PAGES, None, None), P(PAGES, "yh", None), P(PAGES), P(None, PAGES)),
        out_specs=(P(PAGES, None, None), P(PAGES, "yh", None), P(PAGES)),
        check_vma=False,
    )
```

```python
import math

import jax
import jax.numpy as jnp
from jax import lax
from jax.experimental import pallas as pl
from jax.experimental.pallas import tpu as pltpu
from jax.sharding import Mesh
from jax.sharding import PartitionSpec as P

MESH = pl.DeviceIdType.MESH
PAGES = ("yl", "x", "z", "core")

MASKED = -1.0e9
LOGIT_SPAN = 8.0
CENTRE_SHIFT = 0.5
FILL_SHARE = 0.75

NX, NZ = 4, 8
E, LQ, LP = 128, 32, 1024
HALF = LP // 2
ROWS = NX * 2 * LQ
ALL = NZ * ROWS
TILE = 256
F32, BF16 = jnp.float32, jnp.bfloat16

AUX, SIB_PAGE, TILE_Y, FAR_PAGE, SIB_FAR = 0, 1, 2, 3, 5
TILE_Z, TILE_X = 7, 7 + NZ
SUM_X, SUM_Z = TILE_X + NZ, TILE_X + 2 * NZ
FINAL = SUM_Z + NZ
PG_FAR, PG_NEAR, PG_Y, LOSS_SIB, LOSS_Y = range(FINAL + 3, FINAL + 8)
COPIES = LOSS_Y + 1


def dot(left, right, dims=((1,), (0,))):
    return lax.dot_general(left, right, (dims, ((), ())), preferred_element_type=F32)


def offset(rank):
    half, odd = (rank + 1) // 2, rank % 2
    return (odd * half + (1 - odd) * (NZ - half)) % NZ


def kernel(
    q_ref, page_ref, pad_ref, label_ref,
    qg_ref, pg_ref, loss_ref,
    q_all, p_all, p_turned, bias, labels, aux, aux_sib, labels_wide, group_ones,
    raw, weights, tops, sums, labels_rank, scaled, factors, pg_sum,
    qg, qg_sent, in_x, out_z, in_z, fin, in_fin,
    pg_sib, pg_out, pg_far, loss_out, loss_sib, loss_far,
    load_sem, send_sem, recv_sem,
):
    yl, x, z = lax.axis_index("yl"), lax.axis_index("x"), lax.axis_index("z")
    core, yh = lax.axis_index("core"), lax.axis_index("yh")
    oyl, ocore, oyh = 1 - yl, 1 - core, 1 - yh

    loads = [
        pltpu.make_async_copy(q_ref.at[yh], q_all.at[z, x, yl], load_sem.at[0]),
        pltpu.make_async_copy(page_ref.at[0], p_all.at[core, yh], load_sem.at[1]),
        pltpu.make_async_copy(label_ref, labels, load_sem.at[2]),
    ]
    for each in loads:
        each.start()

    def zplus(step):
        return (z + step) % NZ

    def xplus(step):
        return {"x": (x + step) % NX}

    def copy(source, target, index, where):
        return pltpu.make_async_remote_copy(
            src_ref=source,
            dst_ref=target,
            send_sem=send_sem.at[index],
            recv_sem=recv_sem.at[index],
            device_id=where,
            device_id_type=MESH,
        )

    to_sib, to_far, to_y = {"core": ocore}, {"yh": oyh}, {"yl": oyl}
    to_corner = {"yl": oyl, "yh": oyh}

    barrier = pltpu.get_barrier_semaphore()
    partners = [to_sib, to_far, to_y, to_corner]
    partners += [xplus(step) for step in range(1, NX)]
    partners += [{"z": zplus(step)} for step in range(1, NZ)]
    for where in partners:
        pl.semaphore_signal(barrier, inc=1, device_id=where, device_id_type=MESH)

    lane = lax.broadcasted_iota(jnp.int32, (2 * E, ROWS), 1)
    line = lax.broadcasted_iota(jnp.int32, (2 * E, ROWS), 0)
    group_ones[...] = (line // LQ == lane // LQ).astype(F32).astype(BF16)
    for each in loads:
        each.wait()
    row = lax.broadcasted_iota(jnp.int32, (8, 2 * E), 0)
    aux[...] = jnp.where(row == 0, labels[...].astype(F32), pad_ref[0].astype(F32))
    pl.semaphore_wait(barrier, len(partners))

    own_tile = q_all.at[z, x, yl]
    c_tile_y = copy(own_tile, own_tile, TILE_Y, to_y)
    pair = q_all.at[z, x]
    c_tile_z = [
        copy(pair, pair, TILE_Z + rank, {"z": zplus(NZ - offset(rank))}) for rank in range(1, NZ)
    ]
    piece = HALF // 2
    c_far_page = []
    c_sib_far = []
    for part in range(2):
        mine = p_all.at[core, yh, pl.ds(part * piece, piece)]
        c_far_page.append(copy(mine, mine, FAR_PAGE + part, to_far))
        theirs = p_all.at[core, oyh, pl.ds(part * piece, piece)]
        c_sib_far.append(copy(theirs, theirs, SIB_FAR + part, to_sib))
    c_sib_page = copy(p_all.at[core, yh], p_all.at[core, yh], SIB_PAGE, to_sib)
    c_aux = copy(aux, aux_sib, AUX, to_sib)

    def send_x(rank):
        block = q_all.at[zplus(offset(rank)), x]
        for step in range(1, NX):
            copy(block, block, TILE_X + rank, xplus(step)).start()

    def three(rank):
        block = q_all.at[zplus(offset(rank)), pl.ds(0, NX - 1)]
        return copy(block, block, TILE_X + rank, xplus(1))

    c_tile_y.start()
    for each in c_far_page:
        each.start()
    c_aux.start()
    c_sib_page.start()
    c_tile_y.wait_recv()
    for each in c_tile_z:
        each.start()
    send_x(0)

    c_aux.wait_recv()
    position = lax.broadcasted_iota(jnp.int32, (LP, E), 0)
    number = (lane // LQ % 2 * NX + lane // (2 * LQ)) * (NZ * 4) + 2 * core + yh
    wanted = (line // (NZ * 4) == number // (NZ * 4)).astype(F32).astype(BF16)
    block_row = lax.broadcasted_iota(jnp.int32, (8, 2 * E), 0)
    place_in = lax.broadcasted_iota(jnp.int32, (8, 2 * E), 1) % (NZ * 4)
    for place, holder in ((core, aux), (ocore, aux_sib)):
        pad = holder[1:2, 0:E].astype(jnp.int32)
        bias[place] = jnp.where(position < LP - pad, 0.0, MASKED)
        chosen = place_in == block_row * 4 + 2 * core + yh
        spread = jnp.where(chosen, holder[0:1, :], 0.0).astype(BF16)
        labels_wide[place] = dot(spread, wanted)

    for rank in range(1, 3):
        c_tile_z[rank - 1].wait_recv()
        send_x(rank)
    c_sib_page.wait_recv()
    for place in range(2):
        near_half = pl.ds(pl.multiple_of(yh * HALF, HALF), HALF)
        p_turned[place, :, near_half] = p_all[place, yh].astype(F32).T.astype(BF16)
    for rank in range(3, 5):
        c_tile_z[rank - 1].wait_recv()
        send_x(rank)
    for part in range(2):
        c_far_page[part].wait_recv()
        c_sib_far[part].start()
    for part in range(2):
        c_sib_far[part].wait_recv()
    for place in range(2):
        far_half = pl.ds(pl.multiple_of(oyh * HALF, HALF), HALF)
        p_turned[place, :, far_half] = p_all[place, oyh].astype(F32).T.astype(BF16)

    score_scale = E ** (-0.5)
    power = score_scale * math.log2(math.e)
    gain = LOGIT_SPAN / LQ
    centre = LQ * (CENTRE_SHIFT + math.log(FILL_SHARE * LP))

    def forward(rank, carry):
        @pl.when(rank < 3)
        def _():
            later = rank + 5
            copy(pair, pair, TILE_Z + later, to_y).wait_recv()
            send_x(later)

        three(rank).wait_recv()
        block = zplus(offset(rank))
        lanes = pl.ds(pl.multiple_of(rank * ROWS, ROWS), ROWS)
        columns = q_all[block].reshape(ROWS, E).astype(F32).T.astype(BF16)
        for place in range(2):
            top = jnp.full((8, ROWS), -3.0e38, F32)
            for half in range(2):
                scores = dot(p_all[place, half], columns)
                hidden = bias[place, half * HALF : (half + 1) * HALF]
                scores = scores + jnp.concatenate([hidden, hidden], axis=1)
                raw[place, half * HALF : (half + 1) * HALF] = scores
                top = jnp.maximum(top, jnp.max(scores.reshape(HALF // 8, 8, ROWS), axis=0))
            tops[place, pl.ds(rank, 1)] = jnp.max(top, axis=0, keepdims=True)
        for place in range(2):
            total = jnp.zeros((8, ROWS), F32)
            top = tops[place, pl.ds(rank, 1)]
            for tile in range(LP // TILE):
                span = slice(tile * TILE, (tile + 1) * TILE)
                weight = jnp.exp2((raw[place, span] - top) * power)
                weights[place, span, lanes] = weight.astype(BF16)
                total = total + jnp.sum(weight.reshape(TILE // 8, 8, ROWS), axis=0)
            sums[place, pl.ds(rank, 1)] = jnp.sum(total, axis=0, keepdims=True)
        label_rows = [labels_wide[place, pl.ds(block, 1)] for place in range(2)]
        for place in range(2):
            labels_rank[place, pl.ds(rank, 1)] = label_rows[place]
        return carry

    lax.fori_loop(0, NZ, forward, 0)

    losses = []
    for place in range(2):
        smooth = tops[place] * score_scale + jnp.log(sums[place])
        high = smooth.astype(BF16)
        rest = smooth - high.astype(F32)
        middle = rest.astype(BF16)
        low = (rest - middle.astype(F32)).astype(BF16)
        ones = group_ones[...]
        similarity = (dot(low, ones) + dot(middle, ones)) + dot(high, ones)
        sign = 2.0 * labels_rank[place] - 1.0
        lean = -sign * (gain * (similarity - centre))
        small = jnp.exp(-jnp.abs(lean))
        losses.append(jnp.maximum(lean, 0.0) + jnp.log1p(small))
        slope = -gain * sign * (jnp.where(lean >= 0.0, 1.0, small) / (1.0 + small))
        factor = slope / sums[place]
        factors[place] = factor
        turned_factor = factor.T
        for rank in range(NZ):
            rows = q_all[zplus(offset(rank))].reshape(ROWS, E).astype(F32)
            rows = (rows * turned_factor[:, rank : rank + 1]).astype(BF16)
            scaled[place, rank * ROWS : (rank + 1) * ROWS] = rows

    def page_terms(place, half, tile):
        span = pl.ds(pl.multiple_of(half * HALF + tile * TILE, TILE), TILE)
        pg_sum[place, span] = dot(weights[place, span], scaled[place])

    near = pl.ds(pl.multiple_of(yh * HALF, HALF), HALF)
    far = pl.ds(pl.multiple_of(oyh * HALF, HALF), HALF)
    c_pg_far = copy(pg_sum.at[ocore, far], pg_sib.at[0], PG_FAR, to_sib)
    c_pg_near = copy(pg_sum.at[ocore, near], pg_sib.at[1], PG_NEAR, to_sib)
    c_loss_sib = copy(loss_out.at[0], loss_sib, LOSS_SIB, to_sib)
    c_pg_y = copy(pg_out, pg_far, PG_Y, to_far)
    c_loss_y = copy(loss_out.at[1], loss_far, LOSS_Y, to_far)

    for tile in range(HALF // TILE):
        page_terms(ocore, oyh, tile)
    c_pg_far.start()
    mark = lax.broadcasted_iota(jnp.int32, (8, ROWS), 1) % LQ == 0
    first, second = [jnp.sum(jnp.where(mark, each, 0.0), keepdims=True) for each in losses]
    own_loss = jnp.where(core == 0, first, second)
    sib_loss = jnp.where(core == 0, second, first)
    loss_out[0] = jnp.broadcast_to(sib_loss, (8, E))
    c_loss_sib.start()
    for tile in range(HALF // TILE):
        page_terms(core, oyh, tile)

    def backward(step, carry):
        rank = NZ - 1 - step
        lanes = pl.ds(pl.multiple_of(rank * ROWS, ROWS), ROWS)
        gradient = jnp.zeros((E, ROWS), F32)
        for place in range(2):
            gradient = gradient + factors[place, pl.ds(rank, 1)] * dot(
                p_turned[place], weights[place, :, lanes]
            )
        turned = gradient.T.reshape(NX, 2, LQ, E)
        qg[rank] = turned
        qg_sent[rank] = turned.astype(BF16)
        for step_x in range(1, NX):
            copy(
                qg_sent.at[rank, (x + step_x) % NX],
                in_x.at[rank, step_x - 1],
                SUM_X + rank,
                xplus(step_x),
            ).start()

        @pl.when(step == 1)
        def _():
            c_pg_far.wait_recv()
            pg_out[...] = pg_sum[core, far] + pg_sib[0]
            c_pg_y.start()
            c_loss_sib.wait_recv()
            loss_out[1] = jnp.broadcast_to(own_loss, (8, E)) + loss_sib[...]
            c_loss_y.start()

        return carry

    lax.fori_loop(0, NZ, backward, 0)
    def sum_x(step, carry):
        rank = NZ - 1 - step
        copy(qg_sent.at[rank, pl.ds(0, NX - 1)], in_x.at[rank], SUM_X + rank, xplus(1)).wait_recv()
        total = qg[rank, x]
        for slot in range(NX - 1):
            total = total + in_x[rank, slot].astype(F32)
        out_z[rank] = total

        @pl.when(rank > 0)
        def _():
            copy(out_z.at[rank], in_z.at[rank], SUM_Z + rank, {"z": zplus(offset(rank))}).start()

        @pl.when(step % 2 == 1)
        def _():
            late = step // 4
            page_terms(late * core + (1 - late) * ocore, yh, step // 2 % 2)

        @pl.when(step == 3)
        def _():
            c_pg_near.start()

        return carry

    lax.fori_loop(0, NZ, sum_x, 0)
    total = out_z[0]
    for rank in range(NZ - 1, 0, -1):
        copy(out_z.at[rank], in_z.at[rank], SUM_Z + rank, to_y).wait_recv()
        total = total + in_z[rank]
    fin[...] = total * score_scale
    c_fin = [
        copy(fin.at[yl], in_fin.at[2], FINAL + 2, to_far),
        copy(fin.at[oyl], in_fin.at[0], FINAL, to_y),
        copy(fin.at[oyl], in_fin.at[1], FINAL + 1, to_corner),
    ]
    for each in c_fin:
        each.start()
    c_pg_near.wait_recv()
    near_sum = pg_sum[core, near] + pg_sib[1]
    c_loss_y.wait_recv()
    loss_ref[0] = jnp.max(loss_out[1, 0:1, 0:1] + loss_far[0:1, 0:1])
    c_fin[1].wait_recv()
    qg_ref[yh] = fin[yl] + in_fin[0]
    c_fin[2].wait_recv()
    c_fin[0].wait_recv()
    qg_ref[oyh] = in_fin[2] + in_fin[1]
    c_pg_y.wait_recv()
    pg_ref[0] = (near_sum + pg_far[...]) * score_scale

    sent = [c_tile_y, *c_far_page, *c_sib_far, c_sib_page, c_aux, *c_tile_z, *c_fin]
    sent += [c_pg_far, c_pg_near, c_loss_sib, c_pg_y, c_loss_y]
    for each in sent:
        each.wait_send()
    for rank in range(NZ):
        three(rank).wait_send()
        copy(qg_sent.at[rank, pl.ds(0, NX - 1)], in_x.at[rank], SUM_X + rank, xplus(1)).wait_send()
        if rank:
            copy(out_z.at[rank], in_z.at[rank], SUM_Z + rank, to_y).wait_send()


def on_device(queries, pages, pad_counts, labels):
    vmem = pl.BlockSpec(memory_space=pltpu.VMEM)
    smem = pl.BlockSpec(memory_space=pltpu.SMEM)
    hbm = pl.BlockSpec(memory_space=pl.ANY)
    scratch = [
        pltpu.VMEM((NZ, NX, 2, LQ, E), BF16),
        pltpu.VMEM((2, 2, HALF, E), BF16),
        pltpu.VMEM((2, E, LP), BF16),
        pltpu.VMEM((2, LP, E), F32),
        pltpu.VMEM((1, 2 * E), jnp.int32),
        pltpu.VMEM((8, 2 * E), F32),
        pltpu.VMEM((8, 2 * E), F32),
        pltpu.VMEM((2, 8, ROWS), F32),
        pltpu.VMEM((2 * E, ROWS), BF16),
        pltpu.VMEM((2, LP, ROWS), F32),
        pltpu.VMEM((2, LP, ALL), BF16),
        pltpu.VMEM((2, NZ, ROWS), F32),
        pltpu.VMEM((2, NZ, ROWS), F32),
        pltpu.VMEM((2, NZ, ROWS), F32),
        pltpu.VMEM((2, ALL, E), BF16),
        pltpu.VMEM((2, NZ, ROWS), F32),
        pltpu.VMEM((2, LP, E), F32),
        pltpu.VMEM((NZ, NX, 2, LQ, E), F32),
        pltpu.VMEM((NZ, NX, 2, LQ, E), BF16),
        pltpu.VMEM((NZ, NX - 1, 2, LQ, E), BF16),
        pltpu.VMEM((NZ, 2, LQ, E), F32),
        pltpu.VMEM((NZ, 2, LQ, E), F32),
        pltpu.VMEM((2, LQ, E), F32),
        pltpu.VMEM((3, LQ, E), F32),
        pltpu.VMEM((2, HALF, E), F32),
        pltpu.VMEM((HALF, E), F32),
        pltpu.VMEM((HALF, E), F32),
        pltpu.VMEM((2, 8, E), F32),
        pltpu.VMEM((8, E), F32),
        pltpu.VMEM((8, E), F32),
        pltpu.SemaphoreType.DMA((3,)),
        pltpu.SemaphoreType.DMA((COPIES,)),
        pltpu.SemaphoreType.DMA((COPIES,)),
    ]
    flops = 3 * 2 * ALL * (2 * LP) * E
    return pl.pallas_call(
        kernel,
        out_shape=(
            jax.ShapeDtypeStruct(queries.shape, F32),
            jax.ShapeDtypeStruct(pages.shape, F32),
            jax.ShapeDtypeStruct((1,), F32),
        ),
        in_specs=[hbm, hbm, smem, hbm],
        out_specs=(vmem, vmem, smem),
        scratch_shapes=scratch,
        compiler_params=pltpu.CompilerParams(
            collective_id=0, has_side_effects=True, vmem_limit_bytes=56 * 1024 * 1024
        ),
        cost_estimate=pl.CostEstimate(
            flops=flops, bytes_accessed=2 << 20, transcendentals=ALL * 2 * LP
        ),
    )(queries, pages, pad_counts, labels.reshape(1, -1))


def solution(mesh):
    finer = Mesh(mesh.devices.reshape(2, NX, NZ, 2, 2), (*PAGES, "yh"))
    return jax.shard_map(
        on_device,
        mesh=finer,
        in_specs=(P(PAGES, None, None), P(PAGES, "yh", None), P(PAGES), P(None, PAGES)),
        out_specs=(P(PAGES, None, None), P(PAGES, "yh", None), P(PAGES)),
        check_vma=False,
    )
```

```python
import math

import jax
import jax.numpy as jnp
from jax import lax
from jax.experimental import pallas as pl
from jax.experimental.pallas import tpu as pltpu
from jax.sharding import Mesh
from jax.sharding import PartitionSpec as P

MESH = pl.DeviceIdType.MESH
PAGES = ("yl", "x", "z", "core")

MASKED = -1.0e9
LOGIT_SPAN = 8.0
CENTRE_SHIFT = 0.5
FILL_SHARE = 0.75

NX, NZ = 4, 8
E, LQ, LP = 128, 32, 1024
HALF = LP // 2
ROWS = NX * 2 * LQ
ALL = NZ * ROWS
TILE = 256
F32, BF16 = jnp.float32, jnp.bfloat16

AUX, SIB_PAGE, TILE_Y, FAR_PAGE, SIB_FAR = 0, 1, 2, 3, 5
TILE_Z, TILE_X = 7, 7 + NZ
SUM_X, SUM_Z = TILE_X + NZ, TILE_X + 2 * NZ
FINAL = SUM_Z + NZ
PG_FAR, PG_NEAR, PG_Y, LOSS_SIB, LOSS_Y = range(FINAL + 3, FINAL + 8)
COPIES = LOSS_Y + 1


def dot(left, right, dims=((1,), (0,))):
    return lax.dot_general(left, right, (dims, ((), ())), preferred_element_type=F32)


def offset(rank):
    half, odd = (rank + 1) // 2, rank % 2
    return (odd * half + (1 - odd) * (NZ - half)) % NZ


def kernel(
    q_ref, page_ref, pad_ref, label_ref,
    qg_ref, pg_ref, loss_ref,
    q_all, p_all, p_turned, bias, labels, aux, aux_sib, labels_wide, group_ones,
    raw, weights, tops, sums, labels_rank, scaled, factors, pg_sum,
    qg, qg_sent, in_x, out_z, in_z, fin, in_fin,
    pg_sib, pg_out, pg_far, loss_out, loss_sib, loss_far,
    load_sem, send_sem, recv_sem,
):
    yl, x, z = lax.axis_index("yl"), lax.axis_index("x"), lax.axis_index("z")
    core, yh = lax.axis_index("core"), lax.axis_index("yh")
    oyl, ocore, oyh = 1 - yl, 1 - core, 1 - yh

    loads = [
        pltpu.make_async_copy(q_ref.at[yh], q_all.at[z, x, yl], load_sem.at[0]),
        pltpu.make_async_copy(page_ref.at[0], p_all.at[core, yh], load_sem.at[1]),
        pltpu.make_async_copy(label_ref, labels, load_sem.at[2]),
    ]
    for each in loads:
        each.start()

    def zplus(step):
        return (z + step) % NZ

    def xplus(step):
        return {"x": (x + step) % NX}

    def copy(source, target, index, where):
        return pltpu.make_async_remote_copy(
            src_ref=source,
            dst_ref=target,
            send_sem=send_sem.at[index],
            recv_sem=recv_sem.at[index],
            device_id=where,
            device_id_type=MESH,
        )

    to_sib, to_far, to_y = {"core": ocore}, {"yh": oyh}, {"yl": oyl}
    to_corner = {"yl": oyl, "yh": oyh}

    barrier = pltpu.get_barrier_semaphore()
    partners = [to_sib, to_far, to_y, to_corner]
    partners += [xplus(step) for step in range(1, NX)]
    partners += [{"z": zplus(step)} for step in range(1, NZ)]
    for where in partners:
        pl.semaphore_signal(barrier, inc=1, device_id=where, device_id_type=MESH)

    lane = lax.broadcasted_iota(jnp.int32, (2 * E, ROWS), 1)
    line = lax.broadcasted_iota(jnp.int32, (2 * E, ROWS), 0)
    group_ones[...] = (line // LQ == lane // LQ).astype(F32).astype(BF16)
    for each in loads:
        each.wait()
    row = lax.broadcasted_iota(jnp.int32, (8, 2 * E), 0)
    aux[...] = jnp.where(row == 0, labels[...].astype(F32), pad_ref[0].astype(F32))
    pl.semaphore_wait(barrier, len(partners))

    own_tile = q_all.at[z, x, yl]
    c_tile_y = copy(own_tile, own_tile, TILE_Y, to_y)
    pair = q_all.at[z, x]
    c_tile_z = [
        copy(pair, pair, TILE_Z + rank, {"z": zplus(NZ - offset(rank))}) for rank in range(1, NZ)
    ]
    piece = HALF // 2
    c_far_page = []
    c_sib_far = []
    for part in range(2):
        mine = p_all.at[core, yh, pl.ds(part * piece, piece)]
        c_far_page.append(copy(mine, mine, FAR_PAGE + part, to_far))
        theirs = p_all.at[core, oyh, pl.ds(part * piece, piece)]
        c_sib_far.append(copy(theirs, theirs, SIB_FAR + part, to_sib))
    c_sib_page = copy(p_all.at[core, yh], p_all.at[core, yh], SIB_PAGE, to_sib)
    c_aux = copy(aux, aux_sib, AUX, to_sib)

    def send_x(rank):
        block = q_all.at[zplus(offset(rank)), x]
        for step in range(1, NX):
            copy(block, block, TILE_X + rank, xplus(step)).start()

    def three(rank):
        block = q_all.at[zplus(offset(rank)), pl.ds(0, NX - 1)]
        return copy(block, block, TILE_X + rank, xplus(1))

    c_tile_y.start()
    for each in c_far_page:
        each.start()
    c_aux.start()
    c_sib_page.start()
    c_tile_y.wait_recv()
    for each in c_tile_z:
        each.start()
    send_x(0)

    c_aux.wait_recv()
    position = lax.broadcasted_iota(jnp.int32, (LP, E), 0)
    number = (lane // LQ % 2 * NX + lane // (2 * LQ)) * (NZ * 4) + 2 * core + yh
    wanted = (line // (NZ * 4) == number // (NZ * 4)).astype(F32).astype(BF16)
    block_row = lax.broadcasted_iota(jnp.int32, (8, 2 * E), 0)
    place_in = lax.broadcasted_iota(jnp.int32, (8, 2 * E), 1) % (NZ * 4)
    for place, holder in ((core, aux), (ocore, aux_sib)):
        pad = holder[1:2, 0:E].astype(jnp.int32)
        bias[place] = jnp.where(position < LP - pad, 0.0, MASKED)
        chosen = place_in == block_row * 4 + 2 * core + yh
        spread = jnp.where(chosen, holder[0:1, :], 0.0).astype(BF16)
        labels_wide[place] = dot(spread, wanted)

    for rank in range(1, 3):
        c_tile_z[rank - 1].wait_recv()
        send_x(rank)
    c_sib_page.wait_recv()
    for place in range(2):
        near_half = pl.ds(pl.multiple_of(yh * HALF, HALF), HALF)
        p_turned[place, :, near_half] = p_all[place, yh].astype(F32).T.astype(BF16)
    c_far_page[0].wait_recv()
    c_sib_far[0].start()
    for rank in range(3, 5):
        c_tile_z[rank - 1].wait_recv()
        send_x(rank)
    c_far_page[1].wait_recv()
    c_sib_far[1].start()
    for rank in range(5, NZ):
        c_tile_z[rank - 1].wait_recv()
        send_x(rank)
    for part in range(2):
        c_sib_far[part].wait_recv()

    score_scale = E ** (-0.5)
    power = score_scale * math.log2(math.e)
    gain = LOGIT_SPAN / LQ
    centre = LQ * (CENTRE_SHIFT + math.log(FILL_SHARE * LP))

    def scores_of(rank):
        three(rank).wait_recv()
        rows = q_all[zplus(offset(rank))].reshape(ROWS, E)
        found = []
        for place in range(2):
            top = jnp.full((8, ROWS), -3.0e38, F32)
            for half in range(2):
                scores = dot(p_all[place, half], rows, ((1,), (1,)))
                hidden = bias[place, half * HALF : (half + 1) * HALF]
                scores = scores + jnp.concatenate([hidden, hidden], axis=1)
                raw[rank % 2, place, half * HALF : (half + 1) * HALF] = scores
                top = jnp.maximum(top, jnp.max(scores.reshape(HALF // 8, 8, ROWS), axis=0))
            found.append(jnp.max(top, axis=0, keepdims=True))
        return found

    def weights_of(rank, found):
        for place in range(2):
            tops[place, rank : rank + 1] = found[place]
            total = jnp.zeros((8, ROWS), F32)
            for tile in range(LP // TILE):
                span = slice(tile * TILE, (tile + 1) * TILE)
                weight = jnp.exp2((raw[rank % 2, place, span] - found[place]) * power)
                weights[place, span, rank * ROWS : (rank + 1) * ROWS] = weight.astype(BF16)
                total = total + jnp.sum(weight.reshape(TILE // 8, 8, ROWS), axis=0)
            sums[place, rank : rank + 1] = jnp.sum(total, axis=0, keepdims=True)

    found = scores_of(0)
    for rank in range(NZ):
        following = scores_of(rank + 1) if rank + 1 < NZ else None
        weights_of(rank, found)
        found = following
        if rank == 1:
            for place in range(2):
                far_half = pl.ds(pl.multiple_of(oyh * HALF, HALF), HALF)
                p_turned[place, :, far_half] = p_all[place, oyh].astype(F32).T.astype(BF16)
        label_rows = [labels_wide[place, pl.ds(zplus(offset(rank)), 1)] for place in range(2)]
        for place in range(2):
            labels_rank[place, rank : rank + 1] = label_rows[place]

    losses = []
    for place in range(2):
        smooth = tops[place] * score_scale + jnp.log(sums[place])
        high = smooth.astype(BF16)
        rest = smooth - high.astype(F32)
        middle = rest.astype(BF16)
        low = (rest - middle.astype(F32)).astype(BF16)
        ones = group_ones[...]
        similarity = (dot(low, ones) + dot(middle, ones)) + dot(high, ones)
        sign = 2.0 * labels_rank[place] - 1.0
        lean = -sign * (gain * (similarity - centre))
        small = jnp.exp(-jnp.abs(lean))
        losses.append(jnp.maximum(lean, 0.0) + jnp.log1p(small))
        slope = -gain * sign * (jnp.where(lean >= 0.0, 1.0, small) / (1.0 + small))
        factor = slope / sums[place]
        factors[place] = factor

    def page_terms(place, half, tile):
        span = pl.ds(pl.multiple_of(half * HALF + tile * TILE, TILE), TILE)
        pg_sum[place, span] = dot(weights[place, span], scaled[place])

    near = pl.ds(pl.multiple_of(yh * HALF, HALF), HALF)
    far = pl.ds(pl.multiple_of(oyh * HALF, HALF), HALF)
    c_pg_far = copy(pg_sum.at[ocore, far], pg_sib.at[0], PG_FAR, to_sib)
    c_pg_near = copy(pg_sum.at[ocore, near], pg_sib.at[1], PG_NEAR, to_sib)
    c_loss_sib = copy(loss_out.at[0], loss_sib, LOSS_SIB, to_sib)
    c_pg_y = copy(pg_out, pg_far, PG_Y, to_far)
    c_loss_y = copy(loss_out.at[1], loss_far, LOSS_Y, to_far)

    mark = lax.broadcasted_iota(jnp.int32, (8, ROWS), 1) % LQ == 0
    first, second = [jnp.sum(jnp.where(mark, each, 0.0), keepdims=True) for each in losses]
    own_loss = jnp.where(core == 0, first, second)
    sib_loss = jnp.where(core == 0, second, first)
    loss_out[0] = jnp.broadcast_to(sib_loss, (8, E))
    c_loss_sib.start()

    def backward(step, carry):
        rank = NZ - 1 - step
        lanes = pl.ds(pl.multiple_of(rank * ROWS, ROWS), ROWS)
        gradient = jnp.zeros((E, ROWS), F32)
        for place in range(2):
            gradient = gradient + factors[place, pl.ds(rank, 1)] * dot(
                p_turned[place], weights[place, :, lanes]
            )
        turned = gradient.T.reshape(NX, 2, LQ, E)
        qg[rank] = turned
        qg_sent[rank] = turned.astype(BF16)
        for step_x in range(1, NX):
            copy(
                qg_sent.at[rank, (x + step_x) % NX],
                in_x.at[rank, step_x - 1],
                SUM_X + rank,
                xplus(step_x),
            ).start()

        return carry

    lax.fori_loop(0, NZ, backward, 0, unroll=2)
    for place in range(2):
        columns = factors[place].T
        for rank in range(NZ):
            rows = q_all[zplus(offset(rank))].reshape(ROWS, E).astype(F32)
            rows = (rows * columns[:, rank : rank + 1]).astype(BF16)
            scaled[place, rank * ROWS : (rank + 1) * ROWS] = rows

    def sum_x(step, carry):
        rank = NZ - 1 - step
        copy(qg_sent.at[rank, pl.ds(0, NX - 1)], in_x.at[rank], SUM_X + rank, xplus(1)).wait_recv()
        total = qg[rank, x]
        for slot in range(NX - 1):
            total = total + in_x[rank, slot].astype(F32)
        out_z[rank] = total

        @pl.when(rank > 0)
        def _():
            copy(out_z.at[rank], in_z.at[rank], SUM_Z + rank, {"z": zplus(offset(rank))}).start()

        late, near_now = step // 2 % 2, step // 4
        page_terms(
            late * core + (1 - late) * ocore, near_now * yh + (1 - near_now) * oyh, step % 2
        )

        @pl.when(step == 1)
        def _():
            c_pg_far.start()

        @pl.when(step == 4)
        def _():
            c_pg_far.wait_recv()
            pg_out[...] = pg_sum[core, far] + pg_sib[0]
            c_pg_y.start()
            c_loss_sib.wait_recv()
            loss_out[1] = jnp.broadcast_to(own_loss, (8, E)) + loss_sib[...]
            c_loss_y.start()

        @pl.when(step == 5)
        def _():
            c_pg_near.start()

        return carry

    lax.fori_loop(0, NZ, sum_x, 0)
    total = out_z[0]
    for rank in range(NZ - 1, 0, -1):
        copy(out_z.at[rank], in_z.at[rank], SUM_Z + rank, to_y).wait_recv()
        total = total + in_z[rank]
    fin[...] = total * score_scale
    c_fin = [
        copy(fin.at[yl], in_fin.at[2], FINAL + 2, to_far),
        copy(fin.at[oyl], in_fin.at[0], FINAL, to_y),
        copy(fin.at[oyl], in_fin.at[1], FINAL + 1, to_corner),
    ]
    for each in c_fin:
        each.start()
    c_pg_near.wait_recv()
    near_sum = pg_sum[core, near] + pg_sib[1]
    c_loss_y.wait_recv()
    loss_ref[0] = jnp.max(loss_out[1, 0:1, 0:1] + loss_far[0:1, 0:1])
    c_fin[1].wait_recv()
    qg_ref[yh] = fin[yl] + in_fin[0]
    c_fin[2].wait_recv()
    c_fin[0].wait_recv()
    qg_ref[oyh] = in_fin[2] + in_fin[1]
    c_pg_y.wait_recv()
    pg_ref[0] = (near_sum + pg_far[...]) * score_scale

    sent = [c_tile_y, *c_far_page, *c_sib_far, c_sib_page, c_aux, *c_tile_z, *c_fin]
    sent += [c_pg_far, c_pg_near, c_loss_sib, c_pg_y, c_loss_y]
    for each in sent:
        each.wait_send()
    for rank in range(NZ):
        three(rank).wait_send()
        copy(qg_sent.at[rank, pl.ds(0, NX - 1)], in_x.at[rank], SUM_X + rank, xplus(1)).wait_send()
        if rank:
            copy(out_z.at[rank], in_z.at[rank], SUM_Z + rank, to_y).wait_send()


def on_device(queries, pages, pad_counts, labels):
    vmem = pl.BlockSpec(memory_space=pltpu.VMEM)
    smem = pl.BlockSpec(memory_space=pltpu.SMEM)
    hbm = pl.BlockSpec(memory_space=pltpu.HBM)
    scratch = [
        pltpu.VMEM((NZ, NX, 2, LQ, E), BF16),
        pltpu.VMEM((2, 2, HALF, E), BF16),
        pltpu.VMEM((2, E, LP), BF16),
        pltpu.VMEM((2, LP, E), F32),
        pltpu.VMEM((1, 2 * E), jnp.int32),
        pltpu.VMEM((8, 2 * E), F32),
        pltpu.VMEM((8, 2 * E), F32),
        pltpu.VMEM((2, 8, ROWS), F32),
        pltpu.VMEM((2 * E, ROWS), BF16),
        pltpu.VMEM((2, 2, LP, ROWS), F32),
        pltpu.VMEM((2, LP, ALL), BF16),
        pltpu.VMEM((2, NZ, ROWS), F32),
        pltpu.VMEM((2, NZ, ROWS), F32),
        pltpu.VMEM((2, NZ, ROWS), F32),
        pltpu.VMEM((2, ALL, E), BF16),
        pltpu.VMEM((2, NZ, ROWS), F32),
        pltpu.VMEM((2, LP, E), F32),
        pltpu.VMEM((NZ, NX, 2, LQ, E), F32),
        pltpu.VMEM((NZ, NX, 2, LQ, E), BF16),
        pltpu.VMEM((NZ, NX - 1, 2, LQ, E), BF16),
        pltpu.VMEM((NZ, 2, LQ, E), F32),
        pltpu.VMEM((NZ, 2, LQ, E), F32),
        pltpu.VMEM((2, LQ, E), F32),
        pltpu.VMEM((3, LQ, E), F32),
        pltpu.VMEM((2, HALF, E), F32),
        pltpu.VMEM((HALF, E), F32),
        pltpu.VMEM((HALF, E), F32),
        pltpu.VMEM((2, 8, E), F32),
        pltpu.VMEM((8, E), F32),
        pltpu.VMEM((8, E), F32),
        pltpu.SemaphoreType.DMA((3,)),
        pltpu.SemaphoreType.DMA((COPIES,)),
        pltpu.SemaphoreType.DMA((COPIES,)),
    ]
    flops = 3 * 2 * ALL * (2 * LP) * E
    return pl.pallas_call(
        kernel,
        out_shape=(
            jax.ShapeDtypeStruct(queries.shape, F32),
            jax.ShapeDtypeStruct(pages.shape, F32),
            jax.ShapeDtypeStruct((1,), F32),
        ),
        in_specs=[hbm, hbm, smem, hbm],
        out_specs=(vmem, vmem, smem),
        scratch_shapes=scratch,
        compiler_params=pltpu.CompilerParams(
            collective_id=0, has_side_effects=True, vmem_limit_bytes=40 * 1024 * 1024
        ),
        cost_estimate=pl.CostEstimate(
            flops=flops, bytes_accessed=2 << 20, transcendentals=ALL * 2 * LP
        ),
    )(queries, pages, pad_counts, labels.reshape(1, -1))


def solution(mesh):
    finer = Mesh(mesh.devices.reshape(2, NX, NZ, 2, 2), (*PAGES, "yh"))
    return jax.shard_map(
        on_device,
        mesh=finer,
        in_specs=(P(PAGES, None, None), P(PAGES, "yh", None), P(PAGES), P(None, PAGES)),
        out_specs=(P(PAGES, None, None), P(PAGES, "yh", None), P(PAGES)),
        check_vma=False,
    )
```

```python
import math

import jax
import jax.numpy as jnp
from jax import lax
from jax.experimental import pallas as pl
from jax.experimental.pallas import tpu as pltpu
from jax.sharding import Mesh
from jax.sharding import PartitionSpec as P

MESH = pl.DeviceIdType.MESH
PAGES = ("yl", "x", "z", "core")

MASKED = -1.0e9
LOGIT_SPAN = 8.0
CENTRE_SHIFT = 0.5
FILL_SHARE = 0.75

NX, NZ = 4, 8
E, LQ, LP = 128, 32, 1024
HALF = LP // 2
ROWS = NX * 2 * LQ
ALL = NZ * ROWS
TILE = 256
F32, BF16 = jnp.float32, jnp.bfloat16

AUX, SIB_PAGE, TILE_Y, FAR_PAGE, SIB_FAR = 0, 1, 2, 3, 5
TILE_Z, TILE_X = 7, 7 + NZ
SUM_X, SUM_Z = TILE_X + NZ, TILE_X + 2 * NZ
FINAL = SUM_Z + NZ
PG_FAR, PG_NEAR, PG_Y, LOSS_SIB, LOSS_Y = range(FINAL + 3, FINAL + 8)
COPIES = LOSS_Y + 1


def dot(left, right, dims=((1,), (0,))):
    return lax.dot_general(left, right, (dims, ((), ())), preferred_element_type=F32)


def offset(rank):
    half, odd = (rank + 1) // 2, rank % 2
    return (odd * half + (1 - odd) * (NZ - half)) % NZ


def kernel(
    q_ref, page_ref, pad_ref, label_ref,
    qg_ref, pg_ref, loss_ref,
    q_all, p_all, p_turned, bias, labels, aux, aux_sib, labels_wide, group_ones,
    raw, weights, tops, sums, labels_rank, scaled, factors, pg_sum,
    qg, qg_sent, in_x, out_z, in_z, fin, in_fin,
    pg_sib, pg_out, pg_far, loss_out, loss_sib, loss_far,
    load_sem, send_sem, recv_sem,
):
    yl, x, z = lax.axis_index("yl"), lax.axis_index("x"), lax.axis_index("z")
    core, yh = lax.axis_index("core"), lax.axis_index("yh")
    oyl, ocore, oyh = 1 - yl, 1 - core, 1 - yh

    loads = [
        pltpu.make_async_copy(q_ref.at[yh], q_all.at[z, x, yl], load_sem.at[0]),
        pltpu.make_async_copy(page_ref.at[0], p_all.at[core, yh], load_sem.at[1]),
        pltpu.make_async_copy(label_ref, labels, load_sem.at[2]),
    ]
    for each in loads:
        each.start()

    def zplus(step):
        return (z + step) % NZ

    def xplus(step):
        return {"x": (x + step) % NX}

    def copy(source, target, index, where):
        return pltpu.make_async_remote_copy(
            src_ref=source,
            dst_ref=target,
            send_sem=send_sem.at[index],
            recv_sem=recv_sem.at[index],
            device_id=where,
            device_id_type=MESH,
        )

    to_sib, to_far, to_y = {"core": ocore}, {"yh": oyh}, {"yl": oyl}
    to_corner = {"yl": oyl, "yh": oyh}

    barrier = pltpu.get_barrier_semaphore()
    partners = [to_sib, to_far, to_y, to_corner]
    partners += [xplus(step) for step in range(1, NX)]
    partners += [{"z": zplus(step)} for step in range(1, NZ)]
    partners += [{"z": zplus(step), "yl": oyl} for step in range(1, NZ)]
    for where in partners:
        pl.semaphore_signal(barrier, inc=1, device_id=where, device_id_type=MESH)

    lane = lax.broadcasted_iota(jnp.int32, (2 * E, ROWS), 1)
    line = lax.broadcasted_iota(jnp.int32, (2 * E, ROWS), 0)
    group_ones[...] = (line // LQ == lane // LQ).astype(F32).astype(BF16)
    for each in loads:
        each.wait()
    row = lax.broadcasted_iota(jnp.int32, (8, 2 * E), 0)
    aux[...] = jnp.where(row == 0, labels[...].astype(F32), pad_ref[0].astype(F32))
    pl.semaphore_wait(barrier, len(partners))

    own_tile = q_all.at[z, x, yl]
    c_tile_y = copy(own_tile, own_tile, TILE_Y, to_y)
    pair = q_all.at[z, x]
    c_tile_z = [
        copy(pair, pair, TILE_Z + rank, {"z": zplus(NZ - offset(rank))}) for rank in range(1, NZ)
    ]
    piece = HALF // 2
    c_far_page = []
    c_sib_far = []
    for part in range(2):
        mine = p_all.at[core, yh, pl.ds(part * piece, piece)]
        c_far_page.append(copy(mine, mine, FAR_PAGE + part, to_far))
        theirs = p_all.at[core, oyh, pl.ds(part * piece, piece)]
        c_sib_far.append(copy(theirs, theirs, SIB_FAR + part, to_sib))
    c_sib_page = copy(p_all.at[core, yh], p_all.at[core, yh], SIB_PAGE, to_sib)
    c_aux = copy(aux, aux_sib, AUX, to_sib)

    def send_x(rank):
        block = q_all.at[zplus(offset(rank)), x]
        for step in range(1, NX):
            copy(block, block, TILE_X + rank, xplus(step)).start()

    def three(rank):
        block = q_all.at[zplus(offset(rank)), pl.ds(0, NX - 1)]
        return copy(block, block, TILE_X + rank, xplus(1))

    c_tile_y.start()
    for rank in range(1, NZ):
        for line_of in ({}, to_y):
            where = {"z": zplus(NZ - offset(rank)), **line_of}
            copy(own_tile, own_tile, TILE_Z + rank, where).start()
    for each in c_far_page:
        each.start()
    c_aux.start()
    c_sib_page.start()
    c_tile_y.wait_recv()
    send_x(0)

    c_aux.wait_recv()
    position = lax.broadcasted_iota(jnp.int32, (LP, E), 0)
    number = (lane // LQ % 2 * NX + lane // (2 * LQ)) * (NZ * 4) + 2 * core + yh
    wanted = (line // (NZ * 4) == number // (NZ * 4)).astype(F32).astype(BF16)
    block_row = lax.broadcasted_iota(jnp.int32, (8, 2 * E), 0)
    place_in = lax.broadcasted_iota(jnp.int32, (8, 2 * E), 1) % (NZ * 4)
    for place, holder in ((core, aux), (ocore, aux_sib)):
        pad = holder[1:2, 0:E].astype(jnp.int32)
        bias[place] = jnp.where(position < LP - pad, 0.0, MASKED)
        chosen = place_in == block_row * 4 + 2 * core + yh
        spread = jnp.where(chosen, holder[0:1, :], 0.0).astype(BF16)
        labels_wide[place] = dot(spread, wanted)

    for rank in range(1, 3):
        c_tile_z[rank - 1].wait_recv()
        send_x(rank)
    c_sib_page.wait_recv()
    for place in range(2):
        near_half = pl.ds(pl.multiple_of(yh * HALF, HALF), HALF)
        p_turned[place, :, near_half] = p_all[place, yh].astype(F32).T.astype(BF16)
    c_far_page[0].wait_recv()
    c_sib_far[0].start()
    for rank in range(3, 5):
        c_tile_z[rank - 1].wait_recv()
        send_x(rank)
    c_far_page[1].wait_recv()
    c_sib_far[1].start()
    for rank in range(5, NZ):
        c_tile_z[rank - 1].wait_recv()
        send_x(rank)
    for part in range(2):
        c_sib_far[part].wait_recv()

    score_scale = E ** (-0.5)
    power = score_scale * math.log2(math.e)
    gain = LOGIT_SPAN / LQ
    centre = LQ * (CENTRE_SHIFT + math.log(FILL_SHARE * LP))

    def scores_of(rank):
        three(rank).wait_recv()
        rows = q_all[zplus(offset(rank))].reshape(ROWS, E)
        found = []
        for place in range(2):
            top = jnp.full((8, ROWS), -3.0e38, F32)
            for half in range(2):
                scores = dot(p_all[place, half], rows, ((1,), (1,)))
                hidden = bias[place, half * HALF : (half + 1) * HALF]
                scores = scores + jnp.concatenate([hidden, hidden], axis=1)
                raw[rank % 2, place, half * HALF : (half + 1) * HALF] = scores
                top = jnp.maximum(top, jnp.max(scores.reshape(HALF // 8, 8, ROWS), axis=0))
            found.append(jnp.max(top, axis=0, keepdims=True))
        return found

    def weights_of(rank, found):
        for place in range(2):
            tops[place, rank : rank + 1] = found[place]
            total = jnp.zeros((8, ROWS), F32)
            for tile in range(LP // TILE):
                span = slice(tile * TILE, (tile + 1) * TILE)
                weight = jnp.exp2((raw[rank % 2, place, span] - found[place]) * power)
                weights[place, span, rank * ROWS : (rank + 1) * ROWS] = weight.astype(BF16)
                total = total + jnp.sum(weight.reshape(TILE // 8, 8, ROWS), axis=0)
            sums[place, rank : rank + 1] = jnp.sum(total, axis=0, keepdims=True)

    found = scores_of(0)
    for rank in range(NZ):
        following = scores_of(rank + 1) if rank + 1 < NZ else None
        weights_of(rank, found)
        found = following
        if rank == 1:
            for place in range(2):
                far_half = pl.ds(pl.multiple_of(oyh * HALF, HALF), HALF)
                p_turned[place, :, far_half] = p_all[place, oyh].astype(F32).T.astype(BF16)
        label_rows = [labels_wide[place, pl.ds(zplus(offset(rank)), 1)] for place in range(2)]
        for place in range(2):
            labels_rank[place, rank : rank + 1] = label_rows[place]

    losses = []
    for place in range(2):
        smooth = tops[place] * score_scale + jnp.log(sums[place])
        high = smooth.astype(BF16)
        rest = smooth - high.astype(F32)
        middle = rest.astype(BF16)
        low = (rest - middle.astype(F32)).astype(BF16)
        ones = group_ones[...]
        similarity = (dot(low, ones) + dot(middle, ones)) + dot(high, ones)
        sign = 2.0 * labels_rank[place] - 1.0
        lean = -sign * (gain * (similarity - centre))
        small = jnp.exp(-jnp.abs(lean))
        losses.append(jnp.maximum(lean, 0.0) + jnp.log1p(small))
        slope = -gain * sign * (jnp.where(lean >= 0.0, 1.0, small) / (1.0 + small))
        factor = slope / sums[place]
        factors[place] = factor

    def page_terms(place, half, tile):
        span = pl.ds(pl.multiple_of(half * HALF + tile * TILE, TILE), TILE)
        pg_sum[place, span] = dot(weights[place, span], scaled[place])

    near = pl.ds(pl.multiple_of(yh * HALF, HALF), HALF)
    far = pl.ds(pl.multiple_of(oyh * HALF, HALF), HALF)
    c_pg_far = copy(pg_sum.at[ocore, far], pg_sib.at[0], PG_FAR, to_sib)
    c_pg_near = copy(pg_sum.at[ocore, near], pg_sib.at[1], PG_NEAR, to_sib)
    c_loss_sib = copy(loss_out.at[0], loss_sib, LOSS_SIB, to_sib)
    c_pg_y = copy(pg_out, pg_far, PG_Y, to_far)
    c_loss_y = copy(loss_out.at[1], loss_far, LOSS_Y, to_far)

    mark = lax.broadcasted_iota(jnp.int32, (8, ROWS), 1) % LQ == 0
    first, second = [jnp.sum(jnp.where(mark, each, 0.0), keepdims=True) for each in losses]
    own_loss = jnp.where(core == 0, first, second)
    sib_loss = jnp.where(core == 0, second, first)
    loss_out[0] = jnp.broadcast_to(sib_loss, (8, E))
    c_loss_sib.start()

    for place in range(2):
        columns = factors[place].T
        for rank in range(NZ):
            rows = q_all[zplus(offset(rank))].reshape(ROWS, E).astype(F32)
            rows = (rows * columns[:, rank : rank + 1]).astype(BF16)
            scaled[place, rank * ROWS : (rank + 1) * ROWS] = rows

    for tile in range(HALF // TILE):
        page_terms(ocore, oyh, tile)
    c_pg_far.start()

    def backward(step, carry):
        rank = NZ - 1 - step
        lanes = pl.ds(pl.multiple_of(rank * ROWS, ROWS), ROWS)
        gradient = jnp.zeros((E, ROWS), F32)
        for place in range(2):
            gradient = gradient + factors[place, pl.ds(rank, 1)] * dot(
                p_turned[place], weights[place, :, lanes]
            )
        turned = gradient.T.reshape(NX, 2, LQ, E)
        qg[rank] = turned
        qg_sent[rank] = turned.astype(BF16)
        for step_x in range(1, NX):
            copy(
                qg_sent.at[rank, (x + step_x) % NX],
                in_x.at[rank, step_x - 1],
                SUM_X + rank,
                xplus(step_x),
            ).start()

        return carry

    lax.fori_loop(0, NZ, backward, 0, unroll=4)
    def sum_x(step, carry):
        rank = NZ - 1 - step
        copy(qg_sent.at[rank, pl.ds(0, NX - 1)], in_x.at[rank], SUM_X + rank, xplus(1)).wait_recv()
        total = qg[rank, x]
        for slot in range(NX - 1):
            total = total + in_x[rank, slot].astype(F32)
        out_z[rank] = total

        @pl.when(rank > 0)
        def _():
            copy(out_z.at[rank], in_z.at[rank], SUM_Z + rank, {"z": zplus(offset(rank))}).start()

        @pl.when(step < 6)
        def _():
            piece = step + 2
            late, near_now = piece // 2 % 2, piece // 4
            page_terms(
                late * core + (1 - late) * ocore, near_now * yh + (1 - near_now) * oyh, piece % 2
            )

        @pl.when(step == 1)
        def _():
            c_pg_far.wait_recv()
            pg_out[...] = pg_sum[core, far] + pg_sib[0]
            c_pg_y.start()
            c_loss_sib.wait_recv()
            loss_out[1] = jnp.broadcast_to(own_loss, (8, E)) + loss_sib[...]
            c_loss_y.start()

        @pl.when(step == 3)
        def _():
            c_pg_near.start()

        return carry

    lax.fori_loop(0, NZ, sum_x, 0)
    total = out_z[0]
    for rank in range(NZ - 1, 0, -1):
        copy(out_z.at[rank], in_z.at[rank], SUM_Z + rank, to_y).wait_recv()
        total = total + in_z[rank]
    fin[...] = total * score_scale
    c_fin = [
        copy(fin.at[yl], in_fin.at[2], FINAL + 2, to_far),
        copy(fin.at[oyl], in_fin.at[0], FINAL, to_y),
        copy(fin.at[oyl], in_fin.at[1], FINAL + 1, to_corner),
    ]
    for each in c_fin:
        each.start()
    c_pg_near.wait_recv()
    near_sum = pg_sum[core, near] + pg_sib[1]
    c_loss_y.wait_recv()
    loss_ref[0] = jnp.max(loss_out[1, 0:1, 0:1] + loss_far[0:1, 0:1])
    c_fin[1].wait_recv()
    qg_ref[yh] = fin[yl] + in_fin[0]
    c_fin[2].wait_recv()
    c_fin[0].wait_recv()
    qg_ref[oyh] = in_fin[2] + in_fin[1]
    c_pg_y.wait_recv()
    pg_ref[0] = (near_sum + pg_far[...]) * score_scale

    sent = [c_tile_y, *c_far_page, *c_sib_far, c_sib_page, c_aux, *c_tile_z, *c_fin]
    sent += [c_pg_far, c_pg_near, c_loss_sib, c_pg_y, c_loss_y]
    for each in sent:
        each.wait_send()
    for rank in range(NZ):
        three(rank).wait_send()
        copy(qg_sent.at[rank, pl.ds(0, NX - 1)], in_x.at[rank], SUM_X + rank, xplus(1)).wait_send()
        if rank:
            copy(out_z.at[rank], in_z.at[rank], SUM_Z + rank, to_y).wait_send()


def on_device(queries, pages, pad_counts, labels):
    vmem = pl.BlockSpec(memory_space=pltpu.VMEM)
    smem = pl.BlockSpec(memory_space=pltpu.SMEM)
    hbm = pl.BlockSpec(memory_space=pltpu.HBM)
    scratch = [
        pltpu.VMEM((NZ, NX, 2, LQ, E), BF16),
        pltpu.VMEM((2, 2, HALF, E), BF16),
        pltpu.VMEM((2, E, LP), BF16),
        pltpu.VMEM((2, LP, E), F32),
        pltpu.VMEM((1, 2 * E), jnp.int32),
        pltpu.VMEM((8, 2 * E), F32),
        pltpu.VMEM((8, 2 * E), F32),
        pltpu.VMEM((2, 8, ROWS), F32),
        pltpu.VMEM((2 * E, ROWS), BF16),
        pltpu.VMEM((2, 2, LP, ROWS), F32),
        pltpu.VMEM((2, LP, ALL), BF16),
        pltpu.VMEM((2, NZ, ROWS), F32),
        pltpu.VMEM((2, NZ, ROWS), F32),
        pltpu.VMEM((2, NZ, ROWS), F32),
        pltpu.VMEM((2, ALL, E), BF16),
        pltpu.VMEM((2, NZ, ROWS), F32),
        pltpu.VMEM((2, LP, E), F32),
        pltpu.VMEM((NZ, NX, 2, LQ, E), F32),
        pltpu.VMEM((NZ, NX, 2, LQ, E), BF16),
        pltpu.VMEM((NZ, NX - 1, 2, LQ, E), BF16),
        pltpu.VMEM((NZ, 2, LQ, E), F32),
        pltpu.VMEM((NZ, 2, LQ, E), F32),
        pltpu.VMEM((2, LQ, E), F32),
        pltpu.VMEM((3, LQ, E), F32),
        pltpu.VMEM((2, HALF, E), F32),
        pltpu.VMEM((HALF, E), F32),
        pltpu.VMEM((HALF, E), F32),
        pltpu.VMEM((2, 8, E), F32),
        pltpu.VMEM((8, E), F32),
        pltpu.VMEM((8, E), F32),
        pltpu.SemaphoreType.DMA((3,)),
        pltpu.SemaphoreType.DMA((COPIES,)),
        pltpu.SemaphoreType.DMA((COPIES,)),
    ]
    flops = 3 * 2 * ALL * (2 * LP) * E
    return pl.pallas_call(
        kernel,
        out_shape=(
            jax.ShapeDtypeStruct(queries.shape, F32),
            jax.ShapeDtypeStruct(pages.shape, F32),
            jax.ShapeDtypeStruct((1,), F32),
        ),
        in_specs=[hbm, hbm, smem, hbm],
        out_specs=(vmem, vmem, smem),
        scratch_shapes=scratch,
        compiler_params=pltpu.CompilerParams(
            collective_id=0, has_side_effects=True, vmem_limit_bytes=40 * 1024 * 1024
        ),
        cost_estimate=pl.CostEstimate(
            flops=flops, bytes_accessed=2 << 20, transcendentals=ALL * 2 * LP
        ),
    )(queries, pages, pad_counts, labels.reshape(1, -1))


def solution(mesh):
    finer = Mesh(mesh.devices.reshape(2, NX, NZ, 2, 2), (*PAGES, "yh"))
    return jax.shard_map(
        on_device,
        mesh=finer,
        in_specs=(P(PAGES, None, None), P(PAGES, "yh", None), P(PAGES), P(None, PAGES)),
        out_specs=(P(PAGES, None, None), P(PAGES, "yh", None), P(PAGES)),
        check_vma=False,
    )
```

```python
import math

import jax
import jax.numpy as jnp
from jax import lax
from jax.experimental import pallas as pl
from jax.experimental.pallas import tpu as pltpu
from jax.sharding import Mesh
from jax.sharding import PartitionSpec as P

MESH = pl.DeviceIdType.MESH
PAGES = ("yl", "x", "z", "core")

MASKED = -1.0e9
LOGIT_SPAN = 8.0
CENTRE_SHIFT = 0.5
FILL_SHARE = 0.75

NX, NZ = 4, 8
E, LQ, LP = 128, 32, 1024
HALF = LP // 2
ROWS = NX * 2 * LQ
ALL = NZ * ROWS
TILE = 256
F32, BF16 = jnp.float32, jnp.bfloat16

AUX, SIB_PAGE, TILE_Y, FAR_PAGE, SIB_FAR = 0, 1, 2, 3, 5
TILE_Z, TILE_X = 7, 7 + NZ
SUM_X, SUM_Z = TILE_X + NZ, TILE_X + 2 * NZ
FINAL = SUM_Z + NZ
PG_FAR, PG_NEAR, PG_Y, LOSS_SIB, LOSS_Y = range(FINAL + 3, FINAL + 8)
COPIES = LOSS_Y + 1


def dot(left, right, dims=((1,), (0,))):
    return lax.dot_general(left, right, (dims, ((), ())), preferred_element_type=F32)


def offset(rank):
    half, odd = (rank + 1) // 2, rank % 2
    return (odd * half + (1 - odd) * (NZ - half)) % NZ


def kernel(
    in_ref, pad_ref,
    qg_ref, pg_ref, loss_ref,
    q_all, p_all, p_turned, bias, labels, aux, aux_sib, labels_wide, group_ones,
    raw, weights, tops, sums, labels_rank, scaled, factors, pg_sum,
    qg, qg_sent, in_x, out_z, in_z, fin, in_fin,
    pg_sib, pg_out, pg_far, loss_out, loss_sib, loss_far,
    load_sem, send_sem, recv_sem,
):
    yl, x, z = lax.axis_index("yl"), lax.axis_index("x"), lax.axis_index("z")
    core, yh = lax.axis_index("core"), lax.axis_index("yh")
    oyl, ocore, oyh = 1 - yl, 1 - core, 1 - yh

    loads = [
        pltpu.make_async_copy(
            in_ref.at[pl.ds(pl.multiple_of(HALF + yh * LQ, LQ), LQ)],
            q_all.at[z, x, yl],
            load_sem.at[0],
        ),
        pltpu.make_async_copy(in_ref.at[pl.ds(0, HALF)], p_all.at[core, yh], load_sem.at[1]),
        pltpu.make_async_copy(in_ref.at[pl.ds(HALF + 2 * LQ, 16)], labels, load_sem.at[2]),
    ]
    for each in loads:
        each.start()

    def zplus(step):
        return (z + step) % NZ

    def xplus(step):
        return {"x": (x + step) % NX}

    def copy(source, target, index, where):
        return pltpu.make_async_remote_copy(
            src_ref=source,
            dst_ref=target,
            send_sem=send_sem.at[index],
            recv_sem=recv_sem.at[index],
            device_id=where,
            device_id_type=MESH,
        )

    to_sib, to_far, to_y = {"core": ocore}, {"yh": oyh}, {"yl": oyl}
    to_corner = {"yl": oyl, "yh": oyh}

    barrier = pltpu.get_barrier_semaphore()
    partners = [to_sib, to_far, to_y, to_corner]
    partners += [xplus(step) for step in range(1, NX)]
    partners += [{"z": zplus(step)} for step in range(1, NZ)]
    partners += [{"z": zplus(step), "yl": oyl} for step in range(1, NZ)]
    for where in partners:
        pl.semaphore_signal(barrier, inc=1, device_id=where, device_id_type=MESH)

    lane = lax.broadcasted_iota(jnp.int32, (2 * E, ROWS), 1)
    line = lax.broadcasted_iota(jnp.int32, (2 * E, ROWS), 0)
    group_ones[...] = (line // LQ == lane // LQ).astype(F32).astype(BF16)
    for each in loads:
        each.wait()
    row = lax.broadcasted_iota(jnp.int32, (8, 2 * E), 0)
    held = labels[...].astype(F32)
    label_row = jnp.concatenate([held[0:1], held[1:2]], axis=1)
    aux[...] = jnp.where(row == 0, label_row, pad_ref[0].astype(F32))
    pl.semaphore_wait(barrier, len(partners))

    own_tile = q_all.at[z, x, yl]
    c_tile_y = copy(own_tile, own_tile, TILE_Y, to_y)
    pair = q_all.at[z, x]
    c_tile_z = [
        copy(pair, pair, TILE_Z + rank, {"z": zplus(NZ - offset(rank))}) for rank in range(1, NZ)
    ]
    piece = HALF // 2
    c_far_page = []
    c_sib_far = []
    for part in range(2):
        mine = p_all.at[core, yh, pl.ds(part * piece, piece)]
        c_far_page.append(copy(mine, mine, FAR_PAGE + part, to_far))
        theirs = p_all.at[core, oyh, pl.ds(part * piece, piece)]
        c_sib_far.append(copy(theirs, theirs, SIB_FAR + part, to_sib))
    c_sib_page = copy(p_all.at[core, yh], p_all.at[core, yh], SIB_PAGE, to_sib)
    c_aux = copy(aux, aux_sib, AUX, to_sib)

    def send_x(rank):
        block = q_all.at[zplus(offset(rank)), x]
        for step in (2, 1, 3):
            copy(block, block, TILE_X + rank, xplus(step)).start()

    def three(rank):
        block = q_all.at[zplus(offset(rank)), pl.ds(0, NX - 1)]
        return copy(block, block, TILE_X + rank, xplus(1))

    c_tile_y.start()
    for rank in range(NZ - 1, 0, -1):
        for line_of in (to_y, {}):
            where = {"z": zplus(NZ - offset(rank)), **line_of}
            copy(own_tile, own_tile, TILE_Z + rank, where).start()
    for each in c_far_page:
        each.start()
    c_aux.start()
    c_sib_page.start()
    c_tile_y.wait_recv()
    send_x(0)

    c_aux.wait_recv()
    position = lax.broadcasted_iota(jnp.int32, (LP, E), 0)
    number = (lane // LQ % 2 * NX + lane // (2 * LQ)) * (NZ * 4) + 2 * core + yh
    wanted = (line // (NZ * 4) == number // (NZ * 4)).astype(F32).astype(BF16)
    block_row = lax.broadcasted_iota(jnp.int32, (8, 2 * E), 0)
    place_in = lax.broadcasted_iota(jnp.int32, (8, 2 * E), 1) % (NZ * 4)
    for place, holder in ((core, aux), (ocore, aux_sib)):
        pad = holder[1:2, 0:E].astype(jnp.int32)
        bias[place] = jnp.where(position < LP - pad, 0.0, MASKED)
        chosen = place_in == block_row * 4 + 2 * core + yh
        spread = jnp.where(chosen, holder[0:1, :], 0.0).astype(BF16)
        labels_wide[place] = dot(spread, wanted)

    for rank in range(1, 3):
        c_tile_z[rank - 1].wait_recv()
        send_x(rank)
    c_sib_page.wait_recv()
    for place in range(2):
        near_half = pl.ds(pl.multiple_of(yh * HALF, HALF), HALF)
        p_turned[place, :, near_half] = p_all[place, yh].astype(F32).T.astype(BF16)
    c_far_page[0].wait_recv()
    c_sib_far[0].start()
    for rank in range(3, 5):
        c_tile_z[rank - 1].wait_recv()
        send_x(rank)
    c_far_page[1].wait_recv()
    c_sib_far[1].start()
    for rank in range(5, NZ):
        c_tile_z[rank - 1].wait_recv()
        send_x(rank)
    for part in range(2):
        c_sib_far[part].wait_recv()

    score_scale = E ** (-0.5)
    power = score_scale * math.log2(math.e)
    gain = LOGIT_SPAN / LQ
    centre = LQ * (CENTRE_SHIFT + math.log(FILL_SHARE * LP))

    def scores_of(rank):
        three(rank).wait_recv()
        rows = q_all[zplus(offset(rank))].reshape(ROWS, E)
        found = []
        for place in range(2):
            top = jnp.full((8, ROWS), -3.0e38, F32)
            for half in range(2):
                scores = dot(p_all[place, half], rows, ((1,), (1,)))
                hidden = bias[place, half * HALF : (half + 1) * HALF]
                scores = scores + jnp.concatenate([hidden, hidden], axis=1)
                raw[rank % 2, place, half * HALF : (half + 1) * HALF] = scores
                top = jnp.maximum(top, jnp.max(scores.reshape(HALF // 8, 8, ROWS), axis=0))
            found.append(jnp.max(top, axis=0, keepdims=True))
        return found

    def weights_of(rank, found):
        for place in range(2):
            tops[place, rank : rank + 1] = found[place]
            total = jnp.zeros((8, ROWS), F32)
            for tile in range(LP // TILE):
                span = slice(tile * TILE, (tile + 1) * TILE)
                weight = jnp.exp2((raw[rank % 2, place, span] - found[place]) * power)
                weights[place, span, rank * ROWS : (rank + 1) * ROWS] = weight.astype(BF16)
                total = total + jnp.sum(weight.reshape(TILE // 8, 8, ROWS), axis=0)
            sums[place, rank : rank + 1] = jnp.sum(total, axis=0, keepdims=True)

    found = scores_of(0)
    for rank in range(NZ):
        following = scores_of(rank + 1) if rank + 1 < NZ else None
        weights_of(rank, found)
        found = following
        if rank == 1:
            for place in range(2):
                far_half = pl.ds(pl.multiple_of(oyh * HALF, HALF), HALF)
                p_turned[place, :, far_half] = p_all[place, oyh].astype(F32).T.astype(BF16)
        label_rows = [labels_wide[place, pl.ds(zplus(offset(rank)), 1)] for place in range(2)]
        for place in range(2):
            labels_rank[place, rank : rank + 1] = label_rows[place]

    losses = []
    parts = []
    for place in range(2):
        smooth = tops[place] * score_scale + jnp.log(sums[place])
        for _ in range(3):
            part = smooth.astype(BF16).astype(F32)
            parts.append(part)
            smooth = smooth - part
    summed = dot(jnp.concatenate(parts, axis=0).astype(BF16), group_ones[...])
    for place in range(2):
        high, middle, low = [summed[(3 * place + k) * NZ : (3 * place + k + 1) * NZ] for k in range(3)]
        similarity = (low + middle) + high
        sign = 2.0 * labels_rank[place] - 1.0
        lean = -sign * (gain * (similarity - centre))
        small = jnp.exp(-jnp.abs(lean))
        losses.append(jnp.maximum(lean, 0.0) + jnp.log1p(small))
        slope = -gain * sign * (jnp.where(lean >= 0.0, 1.0, small) / (1.0 + small))
        factor = slope / sums[place]
        factors[place] = factor

    def page_terms(place, half, tile):
        span = pl.ds(pl.multiple_of(half * HALF + tile * TILE, TILE), TILE)
        pg_sum[place, span] = dot(weights[place, span], scaled[place])

    near = pl.ds(pl.multiple_of(yh * HALF, HALF), HALF)
    far = pl.ds(pl.multiple_of(oyh * HALF, HALF), HALF)
    c_pg_far = copy(pg_sum.at[ocore, far], pg_sib.at[0], PG_FAR, to_sib)
    c_pg_near = copy(pg_sum.at[ocore, near], pg_sib.at[1], PG_NEAR, to_sib)
    c_loss_sib = copy(loss_out.at[0], loss_sib, LOSS_SIB, to_sib)
    c_pg_y = copy(pg_out, pg_far, PG_Y, to_far)
    c_loss_y = copy(loss_out.at[1], loss_far, LOSS_Y, to_far)

    mark = lax.broadcasted_iota(jnp.int32, (8, ROWS), 1) % LQ == 0
    first, second = [jnp.sum(jnp.where(mark, each, 0.0), keepdims=True) for each in losses]
    own_loss = jnp.where(core == 0, first, second)
    sib_loss = jnp.where(core == 0, second, first)
    loss_out[0] = jnp.broadcast_to(sib_loss, (8, E))
    c_loss_sib.start()

    for place in range(2):
        columns = factors[place].T
        for rank in range(NZ):
            rows = q_all[zplus(offset(rank))].reshape(ROWS, E).astype(F32)
            rows = (rows * columns[:, rank : rank + 1]).astype(BF16)
            scaled[place, rank * ROWS : (rank + 1) * ROWS] = rows

    for tile in range(HALF // TILE):
        page_terms(ocore, oyh, tile)
    c_pg_far.start()

    def backward(step, carry):
        rank = NZ - 1 - step
        lanes = pl.ds(pl.multiple_of(rank * ROWS, ROWS), ROWS)
        gradient = jnp.zeros((E, ROWS), F32)
        for place in range(2):
            gradient = gradient + factors[place, pl.ds(rank, 1)] * dot(
                p_turned[place], weights[place, :, lanes]
            )
        turned = gradient.T.reshape(NX, 2, LQ, E)
        qg[rank] = turned
        qg_sent[rank] = turned.astype(BF16)
        for step_x in (2, 1, 3):
            copy(
                qg_sent.at[rank, (x + step_x) % NX],
                in_x.at[rank, step_x - 1],
                SUM_X + rank,
                xplus(step_x),
            ).start()

        return carry

    lax.fori_loop(0, NZ, backward, 0, unroll=4)
    def sum_x(step, carry):
        rank = NZ - 1 - step
        copy(qg_sent.at[rank, pl.ds(0, NX - 1)], in_x.at[rank], SUM_X + rank, xplus(1)).wait_recv()
        total = qg[rank, x]
        for slot in range(NX - 1):
            total = total + in_x[rank, slot].astype(F32)
        out_z[rank] = total

        @pl.when(rank > 0)
        def _():
            copy(out_z.at[rank], in_z.at[rank], SUM_Z + rank, {"z": zplus(offset(rank))}).start()

        @pl.when(step < 6)
        def _():
            piece = step + 2
            late, near_now = piece // 2 % 2, piece // 4
            page_terms(
                late * core + (1 - late) * ocore, near_now * yh + (1 - near_now) * oyh, piece % 2
            )

        @pl.when(step == 1)
        def _():
            c_pg_far.wait_recv()
            pg_out[...] = pg_sum[core, far] + pg_sib[0]
            c_pg_y.start()
            c_loss_sib.wait_recv()
            loss_out[1] = jnp.broadcast_to(own_loss, (8, E)) + loss_sib[...]
            c_loss_y.start()

        @pl.when(step == 3)
        def _():
            c_pg_near.start()

        return carry

    lax.fori_loop(0, NZ, sum_x, 0)
    total = out_z[0]
    for rank in range(NZ - 1, 0, -1):
        copy(out_z.at[rank], in_z.at[rank], SUM_Z + rank, to_y).wait_recv()
        total = total + in_z[rank]
    fin[...] = total * score_scale
    c_fin = [
        copy(fin.at[yl], in_fin.at[2], FINAL + 2, to_far),
        copy(fin.at[oyl], in_fin.at[0], FINAL, to_y),
        copy(fin.at[oyl], in_fin.at[1], FINAL + 1, to_corner),
    ]
    for each in c_fin:
        each.start()
    c_pg_near.wait_recv()
    near_sum = pg_sum[core, near] + pg_sib[1]
    c_loss_y.wait_recv()
    loss_ref[0] = jnp.max(loss_out[1, 0:1, 0:1] + loss_far[0:1, 0:1])
    c_fin[1].wait_recv()
    qg_ref[yh] = fin[yl] + in_fin[0]
    c_fin[2].wait_recv()
    c_fin[0].wait_recv()
    qg_ref[oyh] = in_fin[2] + in_fin[1]
    c_pg_y.wait_recv()
    pg_ref[0] = (near_sum + pg_far[...]) * score_scale

    sent = [c_tile_y, *c_far_page, *c_sib_far, c_sib_page, c_aux, *c_tile_z, *c_fin]
    sent += [c_pg_far, c_pg_near, c_loss_sib, c_pg_y, c_loss_y]
    for each in sent:
        each.wait_send()
    for rank in range(NZ):
        three(rank).wait_send()
        copy(qg_sent.at[rank, pl.ds(0, NX - 1)], in_x.at[rank], SUM_X + rank, xplus(1)).wait_send()
        if rank:
            copy(out_z.at[rank], in_z.at[rank], SUM_Z + rank, to_y).wait_send()


def on_device(queries, pages, pad_counts, labels):
    vmem = pl.BlockSpec(memory_space=pltpu.VMEM)
    smem = pl.BlockSpec(memory_space=pltpu.SMEM)
    hbm = pl.BlockSpec(memory_space=pltpu.HBM)
    scratch = [
        pltpu.VMEM((NZ, NX, 2, LQ, E), BF16),
        pltpu.VMEM((2, 2, HALF, E), BF16),
        pltpu.VMEM((2, E, LP), BF16),
        pltpu.VMEM((2, LP, E), F32),
        pltpu.VMEM((16, E), BF16),
        pltpu.VMEM((8, 2 * E), F32),
        pltpu.VMEM((8, 2 * E), F32),
        pltpu.VMEM((2, 8, ROWS), F32),
        pltpu.VMEM((2 * E, ROWS), BF16),
        pltpu.VMEM((2, 2, LP, ROWS), F32),
        pltpu.VMEM((2, LP, ALL), BF16),
        pltpu.VMEM((2, NZ, ROWS), F32),
        pltpu.VMEM((2, NZ, ROWS), F32),
        pltpu.VMEM((2, NZ, ROWS), F32),
        pltpu.VMEM((2, ALL, E), BF16),
        pltpu.VMEM((2, NZ, ROWS), F32),
        pltpu.VMEM((2, LP, E), F32),
        pltpu.VMEM((NZ, NX, 2, LQ, E), F32),
        pltpu.VMEM((NZ, NX, 2, LQ, E), BF16),
        pltpu.VMEM((NZ, NX - 1, 2, LQ, E), BF16),
        pltpu.VMEM((NZ, 2, LQ, E), F32),
        pltpu.VMEM((NZ, 2, LQ, E), F32),
        pltpu.VMEM((2, LQ, E), F32),
        pltpu.VMEM((3, LQ, E), F32),
        pltpu.VMEM((2, HALF, E), F32),
        pltpu.VMEM((HALF, E), F32),
        pltpu.VMEM((HALF, E), F32),
        pltpu.VMEM((2, 8, E), F32),
        pltpu.VMEM((8, E), F32),
        pltpu.VMEM((8, E), F32),
        pltpu.SemaphoreType.DMA((3,)),
        pltpu.SemaphoreType.DMA((COPIES,)),
        pltpu.SemaphoreType.DMA((COPIES,)),
    ]
    taken = jnp.concatenate(
        [
            pages.reshape(HALF, E),
            queries.reshape(2 * LQ, E),
            labels.astype(BF16).reshape(2, E),
            jnp.zeros((14, E), BF16),
        ]
    )
    flops = 3 * 2 * ALL * (2 * LP) * E
    return pl.pallas_call(
        kernel,
        out_shape=(
            jax.ShapeDtypeStruct(queries.shape, F32),
            jax.ShapeDtypeStruct(pages.shape, F32),
            jax.ShapeDtypeStruct((1,), F32),
        ),
        in_specs=[hbm, smem],
        out_specs=(vmem, vmem, smem),
        scratch_shapes=scratch,
        compiler_params=pltpu.CompilerParams(
            collective_id=0, has_side_effects=True, vmem_limit_bytes=40 * 1024 * 1024
        ),
        cost_estimate=pl.CostEstimate(
            flops=flops, bytes_accessed=2 << 20, transcendentals=ALL * 2 * LP
        ),
    )(taken, pad_counts)


def solution(mesh):
    finer = Mesh(mesh.devices.reshape(2, NX, NZ, 2, 2), (*PAGES, "yh"))
    return jax.shard_map(
        on_device,
        mesh=finer,
        in_specs=(P(PAGES, None, None), P(PAGES, "yh", None), P(PAGES), P(None, PAGES)),
        out_specs=(P(PAGES, None, None), P(PAGES, "yh", None), P(PAGES)),
        check_vma=False,
    )
```

```python
import math

import jax
import jax.numpy as jnp
from jax import lax
from jax.experimental import pallas as pl
from jax.experimental.pallas import tpu as pltpu
from jax.sharding import Mesh
from jax.sharding import PartitionSpec as P

MESH = pl.DeviceIdType.MESH
PAGES = ("yl", "x", "z", "core")

MASKED = -1.0e9
LOGIT_SPAN = 8.0
CENTRE_SHIFT = 0.5
FILL_SHARE = 0.75

NX, NZ = 4, 8
E, LQ, LP = 128, 32, 1024
HALF = LP // 2
ROWS = NX * 2 * LQ
ALL = NZ * ROWS
TILE = 256
F32, BF16 = jnp.float32, jnp.bfloat16

AUX, SIB_PAGE, TILE_Y, FAR_PAGE, SIB_FAR = 0, 1, 2, 3, 5
TILE_Z, TILE_X = 7, 7 + NZ
SUM_X, SUM_Z = TILE_X + NZ, TILE_X + 2 * NZ
FINAL = SUM_Z + NZ
PG_NEAR, LOSS_SIB, LOSS_Y, PG_FAR, PG_Y = FINAL + 3, FINAL + 4, FINAL + 5, FINAL + 6, FINAL + 8
COPIES = PG_Y + 2


def dot(left, right, dims=((1,), (0,))):
    return lax.dot_general(left, right, (dims, ((), ())), preferred_element_type=F32)


def offset(rank):
    half, odd = (rank + 1) // 2, rank % 2
    return (odd * half + (1 - odd) * (NZ - half)) % NZ


def kernel(
    in_ref, pad_ref,
    qg_ref, pg_ref, loss_ref,
    q_all, p_all, p_turned, bias, labels, aux, aux_sib, labels_wide, group_ones,
    raw, weights, tops, sums, labels_rank, scaled, factors, pg_sum,
    qg, qg_sent, in_x, out_z, in_z, fin, in_fin,
    pg_sib, pg_out, pg_far, loss_out, loss_sib, loss_far,
    load_sem, send_sem, recv_sem,
):
    yl, x, z = lax.axis_index("yl"), lax.axis_index("x"), lax.axis_index("z")
    core, yh = lax.axis_index("core"), lax.axis_index("yh")
    oyl, ocore, oyh = 1 - yl, 1 - core, 1 - yh

    loads = [
        pltpu.make_async_copy(
            in_ref.at[pl.ds(pl.multiple_of(HALF + yh * LQ, LQ), LQ)],
            q_all.at[z, x, yl],
            load_sem.at[0],
        ),
        pltpu.make_async_copy(in_ref.at[pl.ds(0, HALF)], p_all.at[core, yh], load_sem.at[1]),
        pltpu.make_async_copy(in_ref.at[pl.ds(HALF + 2 * LQ, 16)], labels, load_sem.at[2]),
    ]
    for each in loads:
        each.start()

    def zplus(step):
        return (z + step) % NZ

    def xplus(step):
        return {"x": (x + step) % NX}

    def copy(source, target, index, where):
        return pltpu.make_async_remote_copy(
            src_ref=source,
            dst_ref=target,
            send_sem=send_sem.at[index],
            recv_sem=recv_sem.at[index],
            device_id=where,
            device_id_type=MESH,
        )

    to_sib, to_far, to_y = {"core": ocore}, {"yh": oyh}, {"yl": oyl}
    to_corner = {"yl": oyl, "yh": oyh}

    barrier = pltpu.get_barrier_semaphore()
    partners = [to_sib, to_far, to_y, to_corner]
    partners += [xplus(step) for step in range(1, NX)]
    partners += [{"z": zplus(step)} for step in range(1, NZ)]
    partners += [{"z": zplus(step), "yl": oyl} for step in range(1, NZ)]
    for where in partners:
        pl.semaphore_signal(barrier, inc=1, device_id=where, device_id_type=MESH)

    lane = lax.broadcasted_iota(jnp.int32, (2 * E, ROWS), 1)
    line = lax.broadcasted_iota(jnp.int32, (2 * E, ROWS), 0)
    group_ones[...] = (line // LQ == lane // LQ).astype(F32).astype(BF16)
    for each in loads:
        each.wait()
    row = lax.broadcasted_iota(jnp.int32, (8, 2 * E), 0)
    held = labels[...].astype(F32)
    label_row = jnp.concatenate([held[0:1], held[1:2]], axis=1)
    aux[...] = jnp.where(row == 0, label_row, pad_ref[0].astype(F32))
    pl.semaphore_wait(barrier, len(partners))

    own_tile = q_all.at[z, x, yl]
    c_tile_y = copy(own_tile, own_tile, TILE_Y, to_y)
    pair = q_all.at[z, x]
    c_tile_z = [
        copy(pair, pair, TILE_Z + rank, {"z": zplus(NZ - offset(rank))}) for rank in range(1, NZ)
    ]
    piece = HALF // 2
    c_far_page = []
    c_sib_far = []
    for part in range(2):
        mine = p_all.at[core, yh, pl.ds(part * piece, piece)]
        c_far_page.append(copy(mine, mine, FAR_PAGE + part, to_far))
        theirs = p_all.at[core, oyh, pl.ds(part * piece, piece)]
        c_sib_far.append(copy(theirs, theirs, SIB_FAR + part, to_sib))
    c_sib_page = copy(p_all.at[core, yh], p_all.at[core, yh], SIB_PAGE, to_sib)
    c_aux = copy(aux, aux_sib, AUX, to_sib)

    def send_x(rank):
        block = q_all.at[zplus(offset(rank)), x]
        for step in (2, 1, 3):
            copy(block, block, TILE_X + rank, xplus(step)).start()

    def three(rank):
        block = q_all.at[zplus(offset(rank)), pl.ds(0, NX - 1)]
        return copy(block, block, TILE_X + rank, xplus(1))

    c_tile_y.start()
    for rank in range(NZ - 1, 0, -1):
        for line_of in (to_y, {}):
            where = {"z": zplus(NZ - offset(rank)), **line_of}
            copy(own_tile, own_tile, TILE_Z + rank, where).start()
    for each in c_far_page:
        each.start()
    c_aux.start()
    c_sib_page.start()
    c_tile_y.wait_recv()
    send_x(0)

    c_aux.wait_recv()
    position = lax.broadcasted_iota(jnp.int32, (LP, E), 0)
    number = (lane // LQ % 2 * NX + lane // (2 * LQ)) * (NZ * 4) + 2 * core + yh
    wanted = (line // (NZ * 4) == number // (NZ * 4)).astype(F32).astype(BF16)
    block_row = lax.broadcasted_iota(jnp.int32, (8, 2 * E), 0)
    place_in = lax.broadcasted_iota(jnp.int32, (8, 2 * E), 1) % (NZ * 4)
    for place, holder in ((core, aux), (ocore, aux_sib)):
        pad = holder[1:2, 0:E].astype(jnp.int32)
        bias[place] = jnp.where(position < LP - pad, 0.0, MASKED)
        chosen = place_in == block_row * 4 + 2 * core + yh
        spread = jnp.where(chosen, holder[0:1, :], 0.0).astype(BF16)
        labels_wide[place] = dot(spread, wanted)

    for rank in range(1, 3):
        c_tile_z[rank - 1].wait_recv()
        send_x(rank)
    c_sib_page.wait_recv()
    for place in range(2):
        near_half = pl.ds(pl.multiple_of(yh * HALF, HALF), HALF)
        p_turned[place, :, near_half] = p_all[place, yh].astype(F32).T.astype(BF16)
    c_far_page[0].wait_recv()
    c_sib_far[0].start()
    for rank in range(3, 5):
        c_tile_z[rank - 1].wait_recv()
        send_x(rank)
    c_far_page[1].wait_recv()
    c_sib_far[1].start()
    for rank in range(5, NZ):
        c_tile_z[rank - 1].wait_recv()
        send_x(rank)
    for part in range(2):
        c_sib_far[part].wait_recv()

    score_scale = E ** (-0.5)
    power = score_scale * math.log2(math.e)
    gain = LOGIT_SPAN / LQ
    centre = LQ * (CENTRE_SHIFT + math.log(FILL_SHARE * LP))

    def scores_of(rank):
        three(rank).wait_recv()
        rows = q_all[zplus(offset(rank))].reshape(ROWS, E)
        found = []
        for place in range(2):
            top = jnp.full((8, ROWS), -3.0e38, F32)
            for half in range(2):
                scores = dot(p_all[place, half], rows, ((1,), (1,)))
                hidden = bias[place, half * HALF : (half + 1) * HALF]
                scores = scores + jnp.concatenate([hidden, hidden], axis=1)
                raw[rank % 2, place, half * HALF : (half + 1) * HALF] = scores
                top = jnp.maximum(top, jnp.max(scores.reshape(HALF // 8, 8, ROWS), axis=0))
            found.append(jnp.max(top, axis=0, keepdims=True))
        return found

    def weights_of(rank, found):
        for place in range(2):
            tops[place, rank : rank + 1] = found[place]
            total = jnp.zeros((8, ROWS), F32)
            for tile in range(LP // TILE):
                span = slice(tile * TILE, (tile + 1) * TILE)
                weight = jnp.exp2((raw[rank % 2, place, span] - found[place]) * power)
                weights[place, span, rank * ROWS : (rank + 1) * ROWS] = weight.astype(BF16)
                total = total + jnp.sum(weight.reshape(TILE // 8, 8, ROWS), axis=0)
            sums[place, rank : rank + 1] = jnp.sum(total, axis=0, keepdims=True)

    found = scores_of(0)
    for rank in range(NZ):
        following = scores_of(rank + 1) if rank + 1 < NZ else None
        weights_of(rank, found)
        found = following
        if rank == 1:
            for place in range(2):
                far_half = pl.ds(pl.multiple_of(oyh * HALF, HALF), HALF)
                p_turned[place, :, far_half] = p_all[place, oyh].astype(F32).T.astype(BF16)
        label_rows = [labels_wide[place, pl.ds(zplus(offset(rank)), 1)] for place in range(2)]
        for place in range(2):
            labels_rank[place, rank : rank + 1] = label_rows[place]

    losses = []
    parts = []
    for place in range(2):
        smooth = tops[place] * score_scale + jnp.log(sums[place])
        for _ in range(3):
            part = smooth.astype(BF16).astype(F32)
            parts.append(part)
            smooth = smooth - part
    summed = dot(jnp.concatenate(parts, axis=0).astype(BF16), group_ones[...])
    for place in range(2):
        high, middle, low = [summed[(3 * place + k) * NZ : (3 * place + k + 1) * NZ] for k in range(3)]
        similarity = (low + middle) + high
        sign = 2.0 * labels_rank[place] - 1.0
        lean = -sign * (gain * (similarity - centre))
        small = jnp.exp(-jnp.abs(lean))
        losses.append(jnp.maximum(lean, 0.0) + jnp.log1p(small))
        slope = -gain * sign * (jnp.where(lean >= 0.0, 1.0, small) / (1.0 + small))
        factor = slope / sums[place]
        factors[place] = factor

    def page_terms(place, half, tile):
        span = pl.ds(pl.multiple_of(half * HALF + tile * TILE, TILE), TILE)
        pg_sum[place, span] = dot(weights[place, span], scaled[place])

    near = pl.ds(pl.multiple_of(yh * HALF, HALF), HALF)
    def far_tile(tile):
        return pl.ds(pl.multiple_of(oyh * HALF + tile * TILE, TILE), TILE)

    def pg_to_sib(tile):
        rows = pl.ds(pl.multiple_of(tile * TILE, TILE), TILE)
        return copy(pg_sum.at[ocore, far_tile(tile)], pg_sib.at[0, rows], PG_FAR + tile, to_sib)

    def pg_to_far(tile):
        rows = pl.ds(pl.multiple_of(tile * TILE, TILE), TILE)
        return copy(pg_out.at[rows], pg_far.at[rows], PG_Y + tile, to_far)

    c_pg_near = copy(pg_sum.at[ocore, near], pg_sib.at[1], PG_NEAR, to_sib)
    c_loss_sib = copy(loss_out.at[0], loss_sib, LOSS_SIB, to_sib)
    c_loss_y = copy(loss_out.at[1], loss_far, LOSS_Y, to_far)

    mark = lax.broadcasted_iota(jnp.int32, (8, ROWS), 1) % LQ == 0
    first, second = [jnp.sum(jnp.where(mark, each, 0.0), keepdims=True) for each in losses]
    own_loss = jnp.where(core == 0, first, second)
    sib_loss = jnp.where(core == 0, second, first)
    loss_out[0] = jnp.broadcast_to(sib_loss, (8, E))
    c_loss_sib.start()

    for place in range(2):
        columns = factors[place].T
        for rank in range(NZ):
            rows = q_all[zplus(offset(rank))].reshape(ROWS, E).astype(F32)
            rows = (rows * columns[:, rank : rank + 1]).astype(BF16)
            scaled[place, rank * ROWS : (rank + 1) * ROWS] = rows

    for tile in range(HALF // TILE):
        page_terms(ocore, oyh, tile)
        pg_to_sib(tile).start()

    def backward(step, carry):
        rank = NZ - 1 - step
        lanes = pl.ds(pl.multiple_of(rank * ROWS, ROWS), ROWS)
        gradient = jnp.zeros((E, ROWS), F32)
        for place in range(2):
            gradient = gradient + factors[place, pl.ds(rank, 1)] * dot(
                p_turned[place], weights[place, :, lanes]
            )
        turned = gradient.T.reshape(NX, 2, LQ, E)
        qg[rank] = turned
        qg_sent[rank] = turned.astype(BF16)
        for step_x in (2, 1, 3):
            copy(
                qg_sent.at[rank, (x + step_x) % NX],
                in_x.at[rank, step_x - 1],
                SUM_X + rank,
                xplus(step_x),
            ).start()

        return carry

    lax.fori_loop(0, NZ, backward, 0, unroll=4)
    def sum_x(step, carry):
        rank = NZ - 1 - step
        copy(qg_sent.at[rank, pl.ds(0, NX - 1)], in_x.at[rank], SUM_X + rank, xplus(1)).wait_recv()
        total = qg[rank, x]
        for slot in range(NX - 1):
            total = total + in_x[rank, slot].astype(F32)
        out_z[rank] = total

        @pl.when(rank > 0)
        def _():
            copy(out_z.at[rank], in_z.at[rank], SUM_Z + rank, {"z": zplus(offset(rank))}).start()

        @pl.when(step < 6)
        def _():
            piece = step + 2
            late, near_now = piece // 2 % 2, piece // 4
            page_terms(
                late * core + (1 - late) * ocore, near_now * yh + (1 - near_now) * oyh, piece % 2
            )

        @pl.when(step < 2)
        def _():
            rows = pl.ds(pl.multiple_of(step * TILE, TILE), TILE)
            pg_to_sib(step).wait_recv()
            pg_out[rows] = pg_sum[core, far_tile(step)] + pg_sib[0, rows]
            pg_to_far(step).start()

        @pl.when(step == 1)
        def _():
            c_loss_sib.wait_recv()
            loss_out[1] = jnp.broadcast_to(own_loss, (8, E)) + loss_sib[...]
            c_loss_y.start()

        @pl.when(step == 3)
        def _():
            c_pg_near.start()

        return carry

    lax.fori_loop(0, NZ, sum_x, 0)
    total = out_z[0]
    for rank in range(NZ - 1, 0, -1):
        copy(out_z.at[rank], in_z.at[rank], SUM_Z + rank, to_y).wait_recv()
        total = total + in_z[rank]
    fin[...] = total * score_scale
    c_fin = [
        copy(fin.at[yl], in_fin.at[2], FINAL + 2, to_far),
        copy(fin.at[oyl], in_fin.at[0], FINAL, to_y),
        copy(fin.at[oyl], in_fin.at[1], FINAL + 1, to_corner),
    ]
    for each in c_fin:
        each.start()
    c_pg_near.wait_recv()
    near_sum = pg_sum[core, near] + pg_sib[1]
    c_loss_y.wait_recv()
    loss_ref[0] = jnp.max(loss_out[1, 0:1, 0:1] + loss_far[0:1, 0:1])
    c_fin[1].wait_recv()
    qg_ref[yh] = fin[yl] + in_fin[0]
    c_fin[2].wait_recv()
    c_fin[0].wait_recv()
    qg_ref[oyh] = in_fin[2] + in_fin[1]
    for tile in range(HALF // TILE):
        pg_to_far(tile).wait_recv()
    pg_ref[0] = (near_sum + pg_far[...]) * score_scale

    sent = [c_tile_y, *c_far_page, *c_sib_far, c_sib_page, c_aux, *c_tile_z, *c_fin]
    sent += [c_pg_near, c_loss_sib, c_loss_y]
    sent += [each(tile) for each in (pg_to_sib, pg_to_far) for tile in range(HALF // TILE)]
    for each in sent:
        each.wait_send()
    for rank in range(NZ):
        three(rank).wait_send()
        copy(qg_sent.at[rank, pl.ds(0, NX - 1)], in_x.at[rank], SUM_X + rank, xplus(1)).wait_send()
        if rank:
            copy(out_z.at[rank], in_z.at[rank], SUM_Z + rank, to_y).wait_send()


def on_device(queries, pages, pad_counts, labels):
    vmem = pl.BlockSpec(memory_space=pltpu.VMEM)
    smem = pl.BlockSpec(memory_space=pltpu.SMEM)
    hbm = pl.BlockSpec(memory_space=pltpu.HBM)
    scratch = [
        pltpu.VMEM((NZ, NX, 2, LQ, E), BF16),
        pltpu.VMEM((2, 2, HALF, E), BF16),
        pltpu.VMEM((2, E, LP), BF16),
        pltpu.VMEM((2, LP, E), F32),
        pltpu.VMEM((16, E), BF16),
        pltpu.VMEM((8, 2 * E), F32),
        pltpu.VMEM((8, 2 * E), F32),
        pltpu.VMEM((2, 8, ROWS), F32),
        pltpu.VMEM((2 * E, ROWS), BF16),
        pltpu.VMEM((2, 2, LP, ROWS), F32),
        pltpu.VMEM((2, LP, ALL), BF16),
        pltpu.VMEM((2, NZ, ROWS), F32),
        pltpu.VMEM((2, NZ, ROWS), F32),
        pltpu.VMEM((2, NZ, ROWS), F32),
        pltpu.VMEM((2, ALL, E), BF16),
        pltpu.VMEM((2, NZ, ROWS), F32),
        pltpu.VMEM((2, LP, E), F32),
        pltpu.VMEM((NZ, NX, 2, LQ, E), F32),
        pltpu.VMEM((NZ, NX, 2, LQ, E), BF16),
        pltpu.VMEM((NZ, NX - 1, 2, LQ, E), BF16),
        pltpu.VMEM((NZ, 2, LQ, E), F32),
        pltpu.VMEM((NZ, 2, LQ, E), F32),
        pltpu.VMEM((2, LQ, E), F32),
        pltpu.VMEM((3, LQ, E), F32),
        pltpu.VMEM((2, HALF, E), F32),
        pltpu.VMEM((HALF, E), F32),
        pltpu.VMEM((HALF, E), F32),
        pltpu.VMEM((2, 8, E), F32),
        pltpu.VMEM((8, E), F32),
        pltpu.VMEM((8, E), F32),
        pltpu.SemaphoreType.DMA((3,)),
        pltpu.SemaphoreType.DMA((COPIES,)),
        pltpu.SemaphoreType.DMA((COPIES,)),
    ]
    taken = jnp.concatenate(
        [
            pages.reshape(HALF, E),
            queries.reshape(2 * LQ, E),
            labels.astype(BF16).reshape(2, E),
            jnp.zeros((14, E), BF16),
        ]
    )
    flops = 3 * 2 * ALL * (2 * LP) * E
    return pl.pallas_call(
        kernel,
        out_shape=(
            jax.ShapeDtypeStruct(queries.shape, F32),
            jax.ShapeDtypeStruct(pages.shape, F32),
            jax.ShapeDtypeStruct((1,), F32),
        ),
        in_specs=[hbm, smem],
        out_specs=(vmem, vmem, smem),
        scratch_shapes=scratch,
        compiler_params=pltpu.CompilerParams(
            collective_id=0, has_side_effects=True, vmem_limit_bytes=40 * 1024 * 1024
        ),
        cost_estimate=pl.CostEstimate(
            flops=flops, bytes_accessed=2 << 20, transcendentals=ALL * 2 * LP
        ),
    )(taken, pad_counts)


def solution(mesh):
    finer = Mesh(mesh.devices.reshape(2, NX, NZ, 2, 2), (*PAGES, "yh"))
    return jax.shard_map(
        on_device,
        mesh=finer,
        in_specs=(P(PAGES, None, None), P(PAGES, "yh", None), P(PAGES), P(None, PAGES)),
        out_specs=(P(PAGES, None, None), P(PAGES, "yh", None), P(PAGES)),
        check_vma=False,
    )
```
